512 devices in a mesh: tile: 128 (over y, z, core), col: 4 (over x).
Axes of the slice: x: 4, y: 8, z: 8, core: 2. Of those that a mesh axis runs over, the one named last changes fastest.
Arguments:
- block: float32 [128, 294912], P('col', 'tile'), may hold values from -6 to 6
- tiles: float32 [3072, 4, 9216], P('tile'), may hold values from -0.625 to 0.625
- intact: int32 [3072, 4, 96], P('tile'), may hold values 0 or 1
- adjacency: int32 [3072, 4], P('tile'), may hold values from 1 to 3
- stiff_diag: float32 [294912], P('tile'), may hold values from 4 to 40
- cut_low: float32 [1], replicated, may hold values from 14 to 18
- cut_high: float32 [1], replicated, may hold values from 42 to 48
Outputs:
- basis: float32 [128, 294912], P('col', 'tile')
- reduced: float32 [128, 128], replicated
The draws below stay inside these ranges and needn't reach their ends.
All inputs are finite; a program needn't handle non-finite values. No bound on the sum of `intact` on one device may be relied on, other than what follows from the above.
Results may differ from the reference program's by a relative error of at most 0.00017.
Values sent between devices are 32-bit elements; how exact they have to be, the bound alone decides.
A program may use at most 64 MiB of HBM per device.

```python
import math
import jax
import jax.numpy as jnp
from jax import lax

TILE = 96
M = 128
S = 4
R = 3
NBLK = 3072
NDOF = 294912


def touch_ends(array, key, least, high):
    dims = array.shape
    spot = [jax.random.randint(jax.random.fold_in(key, axis), (), 0, dims[axis]) for axis in range(len(dims))]
    array = array.at[tuple(spot)].set(least)
    longest = dims.index(max(dims))
    spot[longest] = (spot[longest] + 1) % dims[longest]
    return array.at[tuple(spot)].set(high)


def block_levels(rng, dims, shards, least, largest):
    def one(position, parts):
        draws = jax.random.uniform(jax.random.fold_in(jax.random.fold_in(rng, 6), position), (parts,), jnp.float32, least / len(shards), largest / len(shards))
        return jnp.repeat(jnp.exp(draws), dims[position] // parts).reshape((-1,) + (1,) * (len(dims) - position - 1))

    gain = one(*shards[0])
    for cut in shards[1:]:
        gain = gain * one(*cut)
    return gain


def noise(rng, shape, scale, bound, pieces=(), kind=jnp.bfloat16):
    entries = scale * jax.random.normal(rng, shape, jnp.float32)
    if pieces:
        entries = entries * block_levels(rng, shape, pieces, -0.22, 0.18)
    return jnp.clip(entries, -bound, bound).astype(kind)


def setup_inputs(seed: int = 0) -> dict:
    seeds = jax.random.split(jax.random.key(seed), 8)
    block = noise(seeds[0], (M, NDOF), 1.0, 6.0, ((0, 4), (1, 128)), jnp.float32)
    tiles = noise(seeds[1], (NBLK, S, TILE * TILE), TILE ** -0.5, 0.625, ((0, 128),), jnp.float32)
    intact = touch_ends((jax.random.randint(seeds[2], (NBLK, S, TILE), 0, 4) < 3).astype(jnp.int32), jax.random.fold_in(seeds[2], 1), 0, 1)
    adjacency = touch_ends(jax.random.randint(seeds[3], (NBLK, S), 1, R + 1), jax.random.fold_in(seeds[3], 1), 1, R).astype(jnp.int32)
    stiff_diag = jnp.clip(jnp.exp(math.log(40.0) - 2.3025851 * jax.random.uniform(seeds[4], (NDOF,), jnp.float32) ** block_levels(seeds[4], (NDOF,), ((0, 128),), -0.2, 0.2)), 4.0, 40.0)
    cut_low = jnp.clip(jax.random.uniform(seeds[5], (1,), jnp.float32, 14.0, 18.0), 14.0, 18.0)
    cut_high = jnp.clip(jax.random.uniform(seeds[6], (1,), jnp.float32, 42.0, 48.0), 42.0, 48.0)
    return {"block": block, "tiles": tiles, "intact": intact, "adjacency": adjacency, "stiff_diag": stiff_diag, "cut_low": cut_low, "cut_high": cut_high}


HIGH = lax.Precision.HIGHEST

def apply_stiffness(rows, coupling, adjacency, stiff_diag):
    count = coupling.shape[0]
    width = coupling.shape[2]
    blocks = rows.reshape(rows.shape[0], count, width)
    extended = jnp.pad(blocks, ((0, 0), (0, R), (0, 0)))
    target = (jnp.arange(count, dtype=jnp.int32)[:, None] + adjacency).astype(jnp.int32)
    neighbours = jnp.take(extended, target, axis=1)
    front = jnp.einsum('jsab,mjsb->mja', coupling, neighbours, precision=HIGH)
    back = jnp.einsum('jsab,mja->mjsb', coupling, blocks, precision=HIGH)
    spread = jnp.zeros(extended.shape, jnp.float32).at[:, target].add(back)[:, :count]
    return stiff_diag[None, :] * rows - (front + spread).reshape(rows.shape)

def inner(left, right):
    return lax.dot_general(left.astype(jnp.float32), right.astype(jnp.float32), (((1,), (1,)), ((), ())), precision=HIGH, preferred_element_type=jnp.float32)

def reference(block, tiles, intact, adjacency, stiff_diag, cut_low, cut_high):
    coupling = intact.astype(jnp.float32)[..., None] * tiles.reshape(NBLK, S, TILE, TILE)
    center = (cut_low[0] + cut_high[0]) / 2.0
    half = (cut_high[0] - cut_low[0]) / 2.0
    first = (apply_stiffness(block, coupling, adjacency, stiff_diag) - center * block) / half
    filtered = 2.0 * (apply_stiffness(first, coupling, adjacency, stiff_diag) - center * first) / half - block
    stiff = apply_stiffness(filtered, coupling, adjacency, stiff_diag)
    gram = inner(filtered, filtered) / NDOF
    proj = inner(stiff, filtered) / NDOF
    lower = jnp.linalg.cholesky(gram)
    inverse = jax.scipy.linalg.solve_triangular(lower, jnp.eye(M, dtype=jnp.float32), lower=True)
    basis = jnp.dot(inverse.astype(jnp.float32), filtered.astype(jnp.float32), precision=HIGH, preferred_element_type=jnp.float32)
    reduced = jnp.dot(jnp.dot(inverse, proj, precision=HIGH), inverse.T, precision=HIGH) / cut_high[0]
    return (basis, reduced)
```

```python
import functools

import jax
import jax.numpy as jnp
from jax import lax
from jax.experimental import pallas as pl
from jax.experimental.pallas import tpu as pltpu
from jax.sharding import PartitionSpec as P

HIGH = lax.Precision.HIGHEST
TILE = 96
LANES = 128
NBLK = 24
REACH = 3
COLS = 32
NCOL = 4
MESH = pl.DeviceIdType.MESH
F32 = jnp.float32
BF16 = jnp.bfloat16


def roll(x, shift):
    return pltpu.roll(x, shift, 1)


def lane_id(rows):
    return lax.broadcasted_iota(jnp.int32, (rows, LANES), 1)


def spread_lanes(x0, x1, x2):
    lane = lane_id(x0.shape[0])
    b1 = jnp.where(lane < 32, roll(x0, 32), roll(x1, 32))
    b2 = jnp.where(lane < 64, roll(x1, 64), roll(x2, 64))
    return x0, b1, b2, roll(x2, 96)


def pack_lanes(b0, b1, b2, b3):
    lane = lane_id(b0.shape[0])
    x0 = jnp.where(lane < 96, b0, roll(b1, 96))
    x1 = jnp.where(lane < 64, roll(b1, 96), roll(b2, 64))
    x2 = jnp.where(lane < 32, roll(b2, 64), roll(b3, 32))
    return x0, x1, x2


def halves(x):
    hi = x.astype(BF16)
    return hi, (x - hi.astype(F32)).astype(BF16)


def contract(left, right, dims, precision=None):
    return lax.dot_general(left, right, (dims, ((), ())), precision=precision, preferred_element_type=F32)


def filter_kernel(
    ntile, zc, block_ref, tiles_ref, mask_ref, adj_ref, diag_ref, low_ref, high_ref,
    rows_out, sums_out,
    tiles_v, merged, ph, plo, v0, v1, v2, vh, acc, ahead, spill, dense, stiff, part, rx1, rx2, sums,
    tile_sem, out_sem, ahead_send, ahead_recv, spill_send, spill_recv, x_send, x_recv, r_send, r_recv,
):
    tile = lax.axis_index("tile")
    col = lax.axis_index("col")
    ny = ntile // zc
    q = lax.rem(tile, zc)
    y = lax.div(tile, zc)
    following = lax.rem(tile + 1, ntile)
    previous = lax.rem(tile + ntile - 1, ntile)
    right = lax.rem(col + 1, NCOL)
    left = lax.rem(col + 3, NCOL)
    opposite = lax.rem(col + 2, NCOL)
    zpeers = [y * zc + lax.rem(q + d, zc) for d in range(1, zc)]
    ypeers = [lax.rem(y + d, ny) * zc + q for d in range(1, ny)]

    barrier = pltpu.get_barrier_semaphore()
    peers = [(t, col) for t in [following, previous] + zpeers + ypeers]
    peers += [(tile, c) for c in (right, left, opposite)]
    for peer in peers:
        pl.semaphore_signal(barrier, inc=1, device_id=peer, device_id_type=MESH)

    chunk = 6
    nchunk = NBLK // chunk
    per = 4 * 72

    def tile_copy(i):
        rows = pl.ds(i * chunk * per, chunk * per)
        return pltpu.make_async_copy(tiles_ref.at[rows], tiles_v.at[rows], tile_sem.at[i])

    for i in range(nchunk):
        tile_copy(i).start()

    valid32 = lane_id(COLS) < TILE
    for g in range(NBLK // 4):
        xs = [block_ref[:, pl.ds((3 * g + i) * LANES, LANES)] for i in range(3)]
        for i, piece in enumerate(spread_lanes(*xs)):
            piece = jnp.where(valid32, piece, 0.0)
            v0[4 * g + i] = piece
            hi, lo = halves(piece)
            vh[4 * g + i, 0:COLS] = hi
            vh[4 * g + i, COLS:2 * COLS] = lo

    valid24 = lane_id(24) < TILE

    def prepare(p, _):
        for par in range(2):
            j = 2 * p + par
            base = 128 * par
            marks = roll(mask_ref[...], 128 - 4 * j)
            slots = []
            for s in range(4):
                xs = [tiles_v[pl.ds(per * j + 4 * f + s, 24, stride=12), :] for f in range(3)]
                pieces = []
                for rho, piece in enumerate(spread_lanes(*xs)):
                    mark = jnp.broadcast_to(marks[24 * rho:24 * rho + 24, s:s + 1], (24, LANES))
                    pieces.append(jnp.where(valid24, piece * mark, 0.0))
                slots.append(pieces)
            for r in range(REACH):
                here = [jnp.where(adj_ref[4 * j + s] == r + 1, 1.0, 0.0).astype(F32) for s in range(4)]
                for rho in range(4):
                    total = slots[0][rho] * here[0]
                    for s in range(1, 4):
                        total += slots[s][rho] * here[s]
                    merged[par, r, pl.ds(rho, 24, stride=4), :] = total
            for r in range(REACH):
                hi, lo = halves(merged[par, r])
                lanes = pl.ds(LANES * (par + r), LANES)
                ph[p, base:base + TILE, lanes] = hi
                plo[p, base:base + TILE, lanes] = lo
            blank = pl.ds(3 * LANES * (1 - par), LANES)
            for ref in (ph, plo):
                ref[p, base:base + TILE, blank] = jnp.zeros((TILE, LANES), BF16)
                ref[p, base + TILE:base + LANES, :] = jnp.zeros((LANES - TILE, 4 * LANES), BF16)
        return 0

    for i in range(nchunk):
        tile_copy(i).wait()
        lax.fori_loop(i * chunk // 2, (i + 1) * chunk // 2, prepare, 0)

    pl.semaphore_wait(barrier, len(peers))

    has_next = tile < ntile - 1
    has_prev = tile > 0
    low = jnp.full((1, LANES), low_ref[0], F32)
    high = jnp.full((1, LANES), high_ref[0], F32)
    center = (low + high) / 2.0
    inv_half = 1.0 / ((high - low) / 2.0)

    def triple(lhs, hi, lo, dims):
        both = contract(lhs, hi, dims)
        return both[:COLS] + both[COLS:] + contract(lhs[:COLS], lo, dims)

    def back(p):
        lhs = jnp.concatenate([vh[2 * p], vh[2 * p + 1]], axis=1)
        res = triple(lhs, ph[p], plo[p], ((1,), (0,)))
        for t in range(4):
            acc[2 * p + 1 + t] += res[:, LANES * t:LANES * (t + 1)]

    def front(p):
        lhs = jnp.concatenate([vh[2 * p + 1 + t] for t in range(4)], axis=1)
        res = triple(lhs, ph[p], plo[p], ((1,), (1,)))
        for t in range(2):
            acc[2 * p + t] += res[:, LANES * t:LANES * (t + 1)]

    def both(p, _):
        back(p)
        front(p)
        return 0

    def apply(a, vec, finish, midway=None):
        to_prev = pltpu.make_async_remote_copy(
            src_ref=vec.at[pl.ds(0, REACH)], dst_ref=ahead.at[a], send_sem=ahead_send.at[a],
            recv_sem=ahead_recv.at[a], device_id=(previous, col), device_id_type=MESH)
        to_prev.start()
        for i in range(NBLK + REACH):
            acc[i] = jnp.zeros((COLS, LANES), F32)
        back(NBLK // 2 - 2)
        back(NBLK // 2 - 1)
        to_next = pltpu.make_async_remote_copy(
            src_ref=acc.at[pl.ds(NBLK, REACH)], dst_ref=spill.at[a], send_sem=spill_send.at[a],
            recv_sem=spill_recv.at[a], device_id=(following, col), device_id_type=MESH)
        to_next.start()
        lax.fori_loop(0, NBLK // 2 - 2, both, 0)
        if midway is not None:
            midway()
        to_prev.wait_recv()
        for i in range(REACH):
            hi, lo = halves(jnp.where(has_next, ahead[a, i], 0.0))
            vh[NBLK + i, 0:COLS] = hi
            vh[NBLK + i, COLS:2 * COLS] = lo
        front(NBLK // 2 - 2)
        front(NBLK // 2 - 1)
        to_next.wait_recv()
        for i in range(REACH):
            acc[i] += jnp.where(has_prev, spill[a, i], 0.0)
        to_prev.wait_send()
        to_next.wait_send()

        def step(i, _):
            finish(i, diag_ref[pl.ds(i, 1), :] * vec[i] - acc[i])
            return 0

        lax.fori_loop(0, NBLK, step, 0)

    def keep(i, value):
        hi, lo = halves(value)
        vh[i, 0:COLS] = hi
        vh[i, COLS:2 * COLS] = lo

    def finish_first(i, kv):
        value = (kv - center * v0[i]) * inv_half
        v1[i] = value
        keep(i, value)

    def finish_filtered(i, kv):
        value = 2.0 * ((kv - center * v1[i]) * inv_half) - v0[i]
        v2[i] = value
        keep(i, value)

    def finish_stiff(i, kv):
        v1[i] = kv

    apply(0, v0, finish_first)
    apply(1, v1, finish_filtered)

    def compact(src, put):
        for g in range(NBLK // 4):
            for i, x in enumerate(pack_lanes(*[src[4 * g + k] for k in range(4)])):
                put((3 * g + i) // 9, pl.ds((3 * g + i) % 9 * LANES, LANES), x)

    def put_dense(h, lanes, x):
        dense[col, h, :, lanes] = x

    def put_stiff(h, lanes, x):
        stiff[h, :, lanes] = x

    def x_copy(i, source, h, to):
        return pltpu.make_async_remote_copy(
            src_ref=dense.at[source, h], dst_ref=dense.at[source, h], send_sem=x_send.at[i],
            recv_sem=x_recv.at[i], device_id=(tile, to), device_id_type=MESH)

    compact(v2, put_dense)
    own = [x_copy(0, col, 0, right), x_copy(1, col, 1, left), x_copy(2, col, 1, right), x_copy(3, col, 0, left)]
    relay = [x_copy(4, left, 0, right), x_copy(5, right, 1, left)]
    for copy in own:
        copy.start()

    def pass_on():
        own[0].wait_recv()
        relay[0].start()
        own[1].wait_recv()
        relay[1].start()

    apply(2, v2, finish_stiff, pass_on)
    compact(v1, put_stiff)
    for copy in own[2:] + relay:
        copy.wait_recv()
    for copy in own + relay:
        copy.wait_send()

    to_out = pltpu.make_async_copy(dense, rows_out, out_sem)
    to_out.start()

    total = jnp.zeros((2 * COLS, LANES), F32)
    for h in range(2):
        lhs = jnp.concatenate([dense[col, h], stiff[h]], axis=0)
        rhs = jnp.concatenate([dense[c, h] for c in range(NCOL)], axis=0)
        total += contract(lhs, rhs, ((1,), (1,)), HIGH)
    total = total * (1.0 / (NBLK * TILE * ntile))

    share = 2 * COLS // zc
    for i in range(zc):
        part[i] = total[share * i:share * (i + 1)]

    def r_copy(i, src, dst, to):
        return pltpu.make_async_remote_copy(
            src_ref=src, dst_ref=dst, send_sem=r_send.at[i], recv_sem=r_recv.at[i],
            device_id=to, device_id_type=MESH)

    def arrived(i, ref):
        copy = r_copy(i, ref, ref, (tile, right))
        copy.wait_recv()
        copy.wait_send()

    for d in range(1, zc):
        r_copy(0, part.at[lax.rem(q + d, zc)], rx1.at[d - 1], (zpeers[d - 1], col)).start()
    arrived(0, rx1)
    mine = part[q]
    for d in range(zc - 1):
        mine += rx1[d]
    rx2[y] = mine
    for t in ypeers:
        r_copy(1, rx2.at[y], rx2.at[y], (t, col)).start()
    arrived(1, rx2.at[pl.ds(0, ny - 1)])
    mine = rx2[0]
    for i in range(1, ny):
        mine += rx2[i]
    sums[col, q] = mine
    for t in zpeers:
        r_copy(2, sums.at[col, q], sums.at[col, q], (t, col)).start()
    arrived(2, sums.at[0, pl.ds(0, zc - 1)])
    for c in (right, left, opposite):
        r_copy(3, sums.at[col], sums.at[col], (tile, c)).start()
    arrived(3, sums.at[pl.ds(0, NCOL - 1)])
    for c in range(NCOL):
        for i in range(zc):
            sums_out[c, share * i:share * (i + 1), :] = sums[c, i]
    to_out.wait()


def ritz_kernel(rows_ref, sums_ref, high_ref, basis_ref, reduced_ref, inv_ref):
    col = lax.axis_index("col")
    m = NCOL * COLS
    groups = m // 8
    lane = lax.broadcasted_iota(jnp.int32, (8, m), 1)
    sub = lax.broadcasted_iota(jnp.int32, (8, m), 0)
    a = [sums_ref[(8 * g) // COLS, pl.ds((8 * g) % COLS, 8), :] for g in range(groups)]
    pivots = []
    for g in range(groups):
        c = [[jnp.broadcast_to(a[h][:, 8 * g + t:8 * g + t + 1], (8, m)) for h in range(g, groups)] for t in range(8)]
        kept = jnp.ones((8, m), F32)
        for t in range(8):
            k = 8 * g + t
            pivot = jnp.broadcast_to(c[t][0][t:t + 1], (8, m))
            kept = jnp.where(sub == t, pivot, kept)
            inv = 1.0 / pivot
            row = jnp.where(lane == k, 1.0, jnp.broadcast_to(a[g][t:t + 1], (8, m)))
            facts = [x * inv for x in c[t]]
            facts[0] = jnp.where(sub > t, facts[0], 0.0)
            for u in range(t + 1, 8):
                same = jnp.broadcast_to(c[t][0][u:u + 1], (8, m))
                c[u] = [x - f * same for x, f in zip(c[u], facts)]
            for h in range(g, groups):
                old = jnp.where((lane == k) & (sub > t) if h == g else lane == k, 0.0, a[h])
                a[h] = old - facts[h - g] * row
        pivots.append(kept)
    for g in range(groups):
        row = sub + 8 * g
        unit = jnp.where(lane < row, a[g], jnp.where(lane == row, 1.0, 0.0))
        inv_ref[8 * g:8 * g + 8, :] = unit / jnp.sqrt(pivots[g])
    mine = inv_ref[pl.ds(col * COLS, COLS), :]
    for h in range(2):
        rhs = jnp.concatenate([rows_ref[c, h] for c in range(NCOL)], axis=0)
        width = rhs.shape[1]
        basis_ref[:, width * h:width * (h + 1)] = contract(mine, rhs, ((1,), (0,)), HIGH)
    inverse = inv_ref[...]
    proj = jnp.concatenate([sums_ref[c, COLS:2 * COLS] for c in range(NCOL)], axis=0)
    half = contract(inverse, proj, ((1,), (0,)), HIGH)
    reduced_ref[...] = contract(half, inverse, ((1,), (1,)), HIGH) / high_ref[0]


def local(ntile, block, tiles, intact, adjacency, stiff_diag, cut_low, cut_high):
    zc = min(16, ntile)
    ny = ntile // zc
    share = 2 * COLS // zc
    flat = tiles.reshape(NBLK, 4, 72, LANES).transpose(0, 2, 1, 3).reshape(NBLK * 4 * 72, LANES)
    mask = intact.astype(F32).reshape(NBLK * 4, 24, 4).transpose(2, 1, 0).reshape(TILE, NBLK * 4)
    mask = jnp.pad(mask, ((0, 0), (0, LANES - NBLK * 4)))
    diag = jnp.pad(stiff_diag.reshape(NBLK, TILE), ((0, 0), (0, LANES - TILE)))
    vm = pl.BlockSpec(memory_space=pltpu.VMEM)
    sm = pl.BlockSpec(memory_space=pltpu.SMEM)
    hbm = pl.BlockSpec(memory_space=pl.ANY)
    npair = NBLK // 2
    dma = pltpu.SemaphoreType.DMA
    vec = pltpu.VMEM((NBLK, COLS, LANES), F32)
    rows, sums = pl.pallas_call(
        functools.partial(filter_kernel, ntile, zc),
        out_shape=(
            jax.ShapeDtypeStruct((NCOL, 2, COLS, 1152), F32),
            jax.ShapeDtypeStruct((NCOL, 2 * COLS, LANES), F32),
        ),
        in_specs=[vm, hbm, vm, sm, vm, sm, sm],
        out_specs=(hbm, vm),
        scratch_shapes=[
            pltpu.VMEM((NBLK * 4 * 72, LANES), F32),
            pltpu.VMEM((2, REACH, TILE, LANES), F32),
            pltpu.VMEM((npair, 2 * LANES, 4 * LANES), BF16),
            pltpu.VMEM((npair, 2 * LANES, 4 * LANES), BF16),
            vec, vec, vec,
            pltpu.VMEM((NBLK + REACH, 2 * COLS, LANES), BF16),
            pltpu.VMEM((NBLK + REACH, COLS, LANES), F32),
            pltpu.VMEM((3, REACH, COLS, LANES), F32),
            pltpu.VMEM((3, REACH, COLS, LANES), F32),
            pltpu.VMEM((NCOL, 2, COLS, 1152), F32),
            pltpu.VMEM((2, COLS, 1152), F32),
            pltpu.VMEM((zc, share, LANES), F32),
            pltpu.VMEM((zc - 1, share, LANES), F32),
            pltpu.VMEM((ny, share, LANES), F32),
            pltpu.VMEM((NCOL, zc, share, LANES), F32),
            dma((4,)), dma, dma((3,)), dma((3,)), dma((3,)), dma((3,)),
            dma((6,)), dma((6,)), dma((4,)), dma((4,)),
        ],
        compiler_params=pltpu.CompilerParams(
            collective_id=0, has_side_effects=True, vmem_limit_bytes=48 * 1024 * 1024),
        name="filter",
    )(block, flat, mask, adjacency.reshape(NBLK * 4), diag, cut_low, cut_high)
    return pl.pallas_call(
        ritz_kernel,
        out_shape=(
            jax.ShapeDtypeStruct((COLS, NBLK * TILE), F32),
            jax.ShapeDtypeStruct((NCOL * COLS, NCOL * COLS), F32),
        ),
        in_specs=[vm, vm, sm],
        out_specs=(vm, vm),
        scratch_shapes=[pltpu.VMEM((NCOL * COLS, NCOL * COLS), F32)],
        compiler_params=pltpu.CompilerParams(vmem_limit_bytes=32 * 1024 * 1024),
        name="ritz",
    )(rows, sums, cut_high)


def solution(mesh):
    in_specs = (
        P("col", "tile"),
        P("tile", None, None),
        P("tile", None, None),
        P("tile", None),
        P("tile"),
        P(),
        P(),
    )
    out_specs = (P("col", "tile"), P())
    return jax.shard_map(
        functools.partial(local, mesh.shape["tile"]), mesh=mesh, in_specs=in_specs, out_specs=out_specs,
        check_vma=False)
```

```python
import functools

import jax
import jax.numpy as jnp
from jax import lax
from jax.experimental import pallas as pl
from jax.experimental.pallas import tpu as pltpu
from jax.sharding import PartitionSpec as P

HIGH = lax.Precision.HIGHEST
TILE = 96
LANES = 128
NBLK = 24
REACH = 3
COLS = 32
NCOL = 4
MESH = pl.DeviceIdType.MESH
F32 = jnp.float32
BF16 = jnp.bfloat16


def aligned(x, step):
    return x if isinstance(x, int) else pl.multiple_of(x, step)


def roll(x, shift):
    return pltpu.roll(x, shift, 1)


def lane_id(rows):
    return lax.broadcasted_iota(jnp.int32, (rows, LANES), 1)


def spread_lanes(x0, x1, x2):
    lane = lane_id(x0.shape[0])
    b1 = jnp.where(lane < 32, roll(x0, 32), roll(x1, 32))
    b2 = jnp.where(lane < 64, roll(x1, 64), roll(x2, 64))
    return x0, b1, b2, roll(x2, 96)


def pack_lanes(b0, b1, b2, b3):
    lane = lane_id(b0.shape[0])
    x0 = jnp.where(lane < 96, b0, roll(b1, 96))
    x1 = jnp.where(lane < 64, roll(b1, 96), roll(b2, 64))
    x2 = jnp.where(lane < 32, roll(b2, 64), roll(b3, 32))
    return x0, x1, x2


def halves(x):
    hi = x.astype(BF16)
    return hi, (x - hi.astype(F32)).astype(BF16)


def contract(left, right, dims, precision=None):
    return lax.dot_general(left, right, (dims, ((), ())), precision=precision, preferred_element_type=F32)


def ritz(col, rows_ref, sums_ref, high_ref, basis_ref, reduced_ref, inv_ref):
    m = NCOL * COLS
    groups = m // 8
    lane = lax.broadcasted_iota(jnp.int32, (8, m), 1)
    sub = lax.broadcasted_iota(jnp.int32, (8, m), 0)
    a = [sums_ref[8 * (g // 4) + g % 4] for g in range(groups)]
    pivots = []
    for g in range(groups):
        c = [[jnp.broadcast_to(a[h][:, 8 * g + t:8 * g + t + 1], (8, m)) for h in range(g, groups)] for t in range(8)]
        kept = jnp.ones((8, m), F32)
        for t in range(8):
            k = 8 * g + t
            pivot = jnp.broadcast_to(c[t][0][t:t + 1], (8, m))
            kept = jnp.where(sub == t, pivot, kept)
            inv = 1.0 / pivot
            row = jnp.where(lane == k, 1.0, jnp.broadcast_to(a[g][t:t + 1], (8, m)))
            facts = [x * inv for x in c[t]]
            facts[0] = jnp.where(sub > t, facts[0], 0.0)
            for u in range(t + 1, 8):
                same = jnp.broadcast_to(c[t][0][u:u + 1], (8, m))
                c[u] = [x - f * same for x, f in zip(c[u], facts)]
            for h in range(g, groups):
                old = jnp.where((lane == k) & (sub > t) if h == g else lane == k, 0.0, a[h])
                a[h] = old - facts[h - g] * row
        pivots.append(kept)
    for g in range(groups):
        row = sub + 8 * g
        unit = jnp.where(lane < row, a[g], jnp.where(lane == row, 1.0, 0.0))
        inv_ref[8 * g:8 * g + 8, :] = unit / jnp.sqrt(pivots[g])
    mine = inv_ref[pl.ds(col * COLS, COLS), :]
    mine = jnp.concatenate(halves(mine), axis=0)
    for g in range(NBLK // 4):
        hi, lo = halves(jnp.concatenate([rows_ref[c, g] for c in range(NCOL)], axis=0))
        width = hi.shape[1]
        both = contract(mine, hi, ((1,), (0,)))
        low = contract(mine[:COLS], lo, ((1,), (0,)))
        basis_ref[:, width * g:width * (g + 1)] = both[:COLS] + (both[COLS:] + low)
    inverse = inv_ref[...]
    proj = jnp.concatenate([sums_ref[8 * (g // 4) + 4 + g % 4] for g in range(groups)], axis=0)
    half = contract(inverse, proj, ((1,), (0,)), HIGH)
    reduced_ref[...] = contract(half, inverse, ((1,), (1,)), HIGH) / high_ref[0]


def filter_kernel(
    ntile, zc, block_ref, tiles_ref, intact_ref, adj_ref, diag_ref, low_ref, high_ref,
    basis_ref, reduced_ref,
    tiles_v, intact_v, block_v, diag_in, marks_k, marks_f, marks_in, marks_v, diag_v, merged, qh, qlo, v0, v1, v2, vh, ahead, spill, spill_out, dense, stiff,
    part, rx1, rx2, sums, inv_v,
    tile_sem, in_sem, ahead_send, ahead_recv, spill_send, spill_recv, x_send, x_recv, r_send, r_recv,
):
    tile = lax.axis_index("tile")
    col = lax.axis_index("col")
    ny = ntile // zc
    q = lax.rem(tile, zc)
    y = lax.div(tile, zc)
    following = lax.rem(tile + 1, ntile)
    previous = lax.rem(tile + ntile - 1, ntile)
    right = lax.rem(col + 1, NCOL)
    left = lax.rem(col + 3, NCOL)
    opposite = lax.rem(col + 2, NCOL)
    zpeers = [(y * zc + lax.rem(q + d, zc), col) for d in range(1, zc)]
    ypeers = [(lax.rem(y + d, ny) * zc + q, col) for d in range(1, ny)]
    core = lax.rem(q, 2)

    def near(dz, c, other):
        return (y * zc + lax.rem(q - core + 2 * dz + zc, zc) + (1 - core if other else core), c)

    spread = [near(dz, c, other) for c in (col, right, left, opposite) for dz in (0, 1, -1, -2)
              for other in (False, True)][1:]

    barrier = pltpu.get_barrier_semaphore()
    peers = [(following, col), (previous, col)] + ypeers + zpeers
    peers += [near(dz, c, other) for c in (right, left, opposite) for dz in (-2, -1, 0, 1, 2)
              for other in (False, True)]

    npair = NBLK // 2
    per = 4 * 72
    chunk = 3

    def tile_copy(i):
        rows = pl.ds(i * 2 * chunk * per, 2 * chunk * per)
        return pltpu.make_async_copy(tiles_ref.at[rows], tiles_v.at[rows], tile_sem.at[i])

    order = (3, 0, 1, 2)
    small = [pltpu.make_async_copy(src, dst, in_sem.at[i]) for i, (src, dst) in enumerate(
        ((intact_ref, intact_v), (block_ref, block_v), (diag_ref, diag_in)))]
    for copy in small:
        copy.start()
    for i in order:
        tile_copy(i).start()
    for peer in peers:
        pl.semaphore_signal(barrier, inc=1, device_id=peer, device_id_type=MESH)

    def window(buf, p, first=0, last=8):
        start = aligned(2 * LANES * p + LANES * first, LANES)
        return vh[buf, :, pl.ds(start, LANES * (last - first))]

    def keep(buf, p, value):
        hi, lo = halves(value)
        lanes = pl.ds(aligned(2 * LANES * p + REACH * LANES, LANES), value.shape[1])
        vh[buf, 0:COLS, lanes] = hi
        vh[buf, COLS:2 * COLS, lanes] = lo

    def pair(p):
        return pl.ds(aligned(2 * LANES * p, 2 * LANES), 2 * LANES)

    merged[...] = jnp.zeros(merged.shape, F32)
    for ref in (qh, qlo):
        for p, w, c in ((0, 0, 0), (0, 1, 0), (0, 2, 0), (0, 1, 1), (0, 2, 1), (1, 0, 0), (npair, 0, 1)):
            ref[p, pl.ds(LANES * w, LANES), pl.ds(LANES * c, LANES)] = jnp.zeros((LANES, LANES), BF16)
    for buf in range(2):
        vh[buf, :, 0:REACH * LANES] = jnp.zeros((2 * COLS, REACH * LANES), BF16)

    nmark = 3 * 4 * LANES
    rows_id = lax.broadcasted_iota(jnp.int32, (16, nmark), 0)
    lanes_id = lax.broadcasted_iota(jnp.int32, (16, nmark), 1)
    slot_at = lax.div(lanes_id, 3 * LANES)
    row_at = lax.div(lax.rem(lanes_id, 3 * LANES), TILE)
    pick = jnp.where(rows_id == 4 * row_at + slot_at, 1.0, 0.0).astype(BF16)
    marks_in[...] = jnp.zeros((LANES, LANES), F32)
    small[0].wait()
    for j in range(NBLK):
        marks_in[4 * j:4 * j + 4, 0:TILE] = intact_v[j].astype(F32)
    marks_v[...] = marks_in[...].T
    lane24 = lane_id(24)

    def gather_marks(j, _):
        total = jnp.zeros((24, LANES), F32)
        for rho in range(4):
            moved = roll(marks_v[pl.ds(rho, 24, stride=4), :], lax.rem(LANES + 4 * rho - 4 * j, LANES))
            total = jnp.where((lane24 >= 4 * rho) & (lane24 < 4 * rho + 4), moved, total)
        marks_k[pl.ds(pl.multiple_of(24 * j, 8), 24), :] = total
        return 0

    lax.fori_loop(0, NBLK, gather_marks, 0, unroll=4)

    def spread_marks(i, _):
        rows = pl.ds(pl.multiple_of(96 * i, 8), 96)
        marks_f[rows, :] = contract(marks_k[rows, 0:16].astype(BF16), pick, ((1,), (0,)))
        return 0

    lax.fori_loop(0, 6, spread_marks, 0, unroll=2)

    small[1].wait()
    valid32 = lane_id(COLS) < TILE
    for g in range(NBLK // 4):
        xs = [block_v[:, pl.ds((3 * g + i) * LANES, LANES)] for i in range(3)]
        for i, piece in enumerate(spread_lanes(*xs)):
            piece = jnp.where(valid32, piece, 0.0)
            v0[:, pl.ds((4 * g + i) * LANES, LANES)] = piece
            hi, lo = halves(piece)
            lanes = pl.ds((4 * g + i + REACH) * LANES, LANES)
            vh[0, 0:COLS, lanes] = hi
            vh[0, COLS:2 * COLS, lanes] = lo
    small[2].wait()
    xs = [diag_in[pl.ds(i, NBLK // 4, stride=3), :] for i in range(3)]
    for i, piece in enumerate(spread_lanes(*xs)):
        diag_v[pl.ds(i, NBLK // 4, stride=4), :] = piece

    pl.semaphore_wait(barrier, len(peers))

    def ahead_copy(a, vec):
        return pltpu.make_async_remote_copy(
            src_ref=vec.at[:, pl.ds(0, REACH * LANES)], dst_ref=ahead.at[a], send_sem=ahead_send.at[a],
            recv_sem=ahead_recv.at[a], device_id=(previous, col), device_id_type=MESH)

    ahead_copy(0, v0).start()

    valid24 = lane_id(24) < TILE

    def prepare(p):
        for par in range(2):
            j = 2 * p + par
            rows = pl.ds(24 * j, 24)
            slots = []
            for s in range(4):
                xs = [tiles_v[pl.ds(per * j + 4 * f + s, 24, stride=12), :] for f in range(3)]
                slots.append([x * marks_f[rows, pl.ds((3 * s + f) * LANES, LANES)] for f, x in enumerate(xs)])
            for r in range(REACH):
                here = [jnp.where(adj_ref[s, j] == r + 1, 1.0, 0.0).astype(F32) for s in range(4)]
                xs = []
                for f in range(3):
                    xs.append((slots[0][f] * here[0] + slots[1][f] * here[1])
                              + (slots[2][f] * here[2] + slots[3][f] * here[3]))
                for rho, piece in enumerate(spread_lanes(*xs)):
                    merged[par, r, pl.ds(rho, 24, stride=4), :] = jnp.where(valid24, piece, 0.0)
            for r in range(REACH):
                value = merged[par, r]
                target = par + r + 1
                back_rows = pl.ds(LANES * (par + 3 - 2 * (target // 2)), LANES)
                back_lanes = pl.ds(LANES * (target % 2), LANES)
                hi, lo = halves(value)
                qh[p + target // 2, back_rows, back_lanes] = hi
                qlo[p + target // 2, back_rows, back_lanes] = lo
                front_rows = pl.ds(LANES * (target + 3), LANES)
                hi, lo = halves(value.T)
                qh[p, front_rows, pl.ds(LANES * par, LANES)] = hi
                qlo[p, front_rows, pl.ds(LANES * par, LANES)] = lo
        for ref in (qh, qlo):
            for w, c in ((3, 0), (7, 0), (0, 1), (4, 1)):
                ref[p, pl.ds(LANES * w, LANES), pl.ds(LANES * c, LANES)] = jnp.zeros((LANES, LANES), BF16)

    has_next = tile < ntile - 1
    has_prev = tile > 0
    low = jnp.full((1, 2 * LANES), low_ref[0], F32)
    high = jnp.full((1, 2 * LANES), high_ref[0], F32)
    center = (low + high) / 2.0
    inv_half = 1.0 / ((high - low) / 2.0)

    def product(lhs, hi, lo):
        both = contract(lhs, hi, ((1,), (0,)))
        return both[:COLS] + both[COLS:] + contract(lhs[:COLS], lo, ((1,), (0,)))

    def couple(buf, p, first=0, last=8):
        rows = pl.ds(LANES * first, LANES * (last - first))
        return product(window(buf, p, first, last), qh[p, rows, :], qlo[p, rows, :])

    def spill_copy(a):
        return pltpu.make_async_remote_copy(
            src_ref=spill_out.at[a], dst_ref=spill.at[a], send_sem=spill_send.at[a],
            recv_sem=spill_recv.at[a], device_id=(following, col), device_id_type=MESH)

    def send_spill(a, buf):
        spill_out[a, :, 0:2 * LANES] = couple(buf, npair, 0, 3)
        tail = window(buf, npair, 1, 3)[:, LANES:2 * LANES]
        spill_out[a, :, 2 * LANES:3 * LANES] = product(
            tail, qh[npair + 1, 0:LANES, 0:LANES], qlo[npair + 1, 0:LANES, 0:LANES])
        spill_copy(a).start()

    def stiffness(vec, p, res):
        lanes = pair(p)
        d = jnp.concatenate([diag_v[pl.ds(2 * p, 1), :], diag_v[pl.ds(2 * p + 1, 1), :]], axis=1)
        return d * vec[:, lanes] - res

    def inside(buf, vec, finish, p):
        finish(p, stiffness(vec, p, couple(buf, p)))
        return 0

    def apply(a, buf, vec, finish, hook=None, first=2):
        lax.fori_loop(first, npair - 2, lambda p, _: inside(buf, vec, finish, p), 0, unroll=2)
        if hook is not None:
            hook()
        heads = [couple(buf, p) for p in (0, 1)]
        tails = [couple(buf, npair - 2, 0, 6), couple(buf, npair - 1, 0, 4)]
        ahead_copy(a, vec).wait_recv()
        keep(buf, npair, jnp.where(has_next, ahead[a], 0.0))
        tails[0] += couple(buf, npair - 2, 6, 8)
        tails[1] += couple(buf, npair - 1, 4, 8)
        for i in range(2):
            finish(npair - 2 + i, stiffness(vec, npair - 2 + i, tails[i]))
        spill_copy(a).wait_recv()
        extra = jnp.where(has_prev, spill[a], 0.0)
        heads[0] += extra[:, 0:2 * LANES]
        heads[1] += jnp.concatenate([extra[:, 2 * LANES:], jnp.zeros((COLS, LANES), F32)], axis=1)
        for i in range(2):
            finish(i, stiffness(vec, i, heads[i]))
        ahead_copy(a, vec).wait_send()
        spill_copy(a).wait_send()

    def finish_first(p, kv):
        lanes = pair(p)
        value = (kv - center * v0[:, lanes]) * inv_half
        v1[:, lanes] = value
        keep(1, p, value)

    def finish_filtered(p, kv):
        lanes = pair(p)
        value = 2.0 * ((kv - center * v1[:, lanes]) * inv_half) - v0[:, lanes]
        v2[:, lanes] = value
        keep(0, p, value)

    def finish_stiff(p, kv):
        v1[:, pair(p)] = kv

    def compact(src, g):
        return pack_lanes(*[src[:, pl.ds((4 * g + k) * LANES, LANES)] for k in range(4)])

    ngroup = NBLK // 4
    lower = (0, 1, 2)
    upper = (3, 4, 5)

    def x_copy(i, source, g, to):
        return pltpu.make_async_remote_copy(
            src_ref=dense.at[source, g], dst_ref=dense.at[source, g], send_sem=x_send.at[i],
            recv_sem=x_recv.at[i], device_id=(tile, to), device_id_type=MESH)

    def to_right(g, source=None):
        if source is None:
            return x_copy(g, col, g, right)
        return x_copy(2 * ngroup + g, source, g, right)

    def to_left(g, source=None):
        if source is None:
            return x_copy(ngroup + g, col, g, left)
        return x_copy(2 * ngroup + g, source, g, left)

    def send_groups(rights, lefts):
        for g in sorted(set(rights + lefts)):
            for i, x in enumerate(compact(v2, g)):
                dense[col, g, :, LANES * i:LANES * (i + 1)] = x
        for a, b in zip(rights, lefts):
            to_right(a).start()
            to_left(b).start()

    for n, i in enumerate(order):
        tile_copy(i).wait()
        for p in range(i * chunk, (i + 1) * chunk):
            prepare(p)
            if 2 < p < npair - chunk:
                inside(0, v0, finish_first, p - 1)
        if n == 0:
            send_spill(0, 0)
    apply(0, 0, v0, finish_first, first=npair - chunk - 1)
    ahead_copy(1, v1).start()
    send_spill(1, 1)
    apply(1, 1, v1, finish_filtered, lambda: send_groups((1, 2, 3, 4), (4, 3, 2, 1)))
    ahead_copy(2, v2).start()
    send_spill(2, 0)
    send_groups((0, 5), (5, 0))

    def pass_on():
        for a, b in ((1, 4), (2, 3), (0, 5)):
            to_right(a).wait_recv()
            to_right(a, left).start()
            to_left(b).wait_recv()
            to_left(b, right).start()

    apply(2, 0, v2, finish_stiff)
    pass_on()
    for g in range(ngroup):
        for i, x in enumerate(compact(v1, g)):
            stiff[g, :, LANES * i:LANES * (i + 1)] = x

    def split_rows(g):
        hi_f, lo_f = halves(dense[col, g])
        hi_s, lo_s = halves(stiff[g])
        return jnp.concatenate([hi_f, hi_s, lo_f, lo_s], axis=0)

    own = [split_rows(g) for g in range(ngroup)]

    def against(source, groups):
        lhs = jnp.concatenate([own[g] for g in groups], axis=1)
        parts = [halves(dense[source, g]) for g in groups]
        rhs = jnp.concatenate([jnp.concatenate([x[i] for x in parts], axis=1) for i in range(2)], axis=0)
        res = contract(lhs, rhs, ((1,), (1,)))
        half = 2 * COLS
        return res[:half, :COLS] + res[half:, :COLS] + (res[:half, COLS:] + res[half:, COLS:])

    mine = against(col, lower + upper)
    of_left = against(left, lower)
    of_right = against(right, upper)
    for g in upper:
        to_right(g).wait_recv()
    of_left += against(left, upper)
    for g in lower:
        to_left(g).wait_recv()
    of_right += against(right, lower)
    of_opposite = jnp.zeros((2 * COLS, COLS), F32)
    for groups in ((1, 2, 3, 4), (0, 5)):
        for g in groups:
            (to_right(g, left) if g in lower else to_left(g, right)).wait_recv()
        of_opposite += against(opposite, groups)
    total = jnp.concatenate([mine, of_right, of_opposite, of_left], axis=1)
    total = roll(total, COLS * col) * (1.0 / (NBLK * TILE * ntile))

    nshare = 8
    share = 2 * COLS // nshare
    for i in range(nshare):
        part[i] = total[share * i:share * (i + 1)]

    def r_copy(i, src, dst, to):
        return pltpu.make_async_remote_copy(
            src_ref=src, dst_ref=dst, send_sem=r_send.at[i], recv_sem=r_recv.at[i],
            device_id=to, device_id_type=MESH)

    def arrived(i, ref):
        copy = r_copy(i, ref, ref, (tile, right))
        copy.wait_recv()
        copy.wait_send()

    for d in range(1, zc):
        r_copy(0, part.at[lax.rem(q + d, nshare)], rx1.at[q], zpeers[d - 1]).start()
    own_share = lax.rem(q, nshare)
    rx1[q] = part[own_share]
    arrived(0, rx1.at[pl.ds(0, zc - 1)])
    mine = rx1[0]
    for i in range(1, zc):
        mine += rx1[i]
    rx2[y] = mine
    for peer in ypeers:
        r_copy(1, rx2.at[y], rx2.at[y], peer).start()
    arrived(1, rx2.at[pl.ds(0, ny - 1)])
    mine = rx2[0]
    for i in range(1, ny):
        mine += rx2[i]
    here = nshare * col + own_share
    sums[here] = mine
    for peer in spread:
        r_copy(2, sums.at[here], sums.at[here], peer).start()
    arrived(2, sums.at[pl.ds(0, NCOL * nshare - 1)])
    for g in range(ngroup):
        to_right(g).wait_send()
        to_left(g).wait_send()
        (to_right(g, left) if g in lower else to_left(g, right)).wait_send()
    ritz(col, dense, sums, high_ref, basis_ref, reduced_ref, inv_v)


def local(ntile, block, tiles, intact, adjacency, stiff_diag, cut_low, cut_high):
    zc = min(16, ntile)
    ny = ntile // zc
    share = 2 * COLS // 8
    flat = tiles.reshape(NBLK, 4, 72, LANES).transpose(0, 2, 1, 3).reshape(NBLK * 4 * 72, LANES)
    diag = stiff_diag.reshape(NBLK * TILE // LANES, LANES)
    vm = pl.BlockSpec(memory_space=pltpu.VMEM)
    sm = pl.BlockSpec(memory_space=pltpu.SMEM)
    hbm = pl.BlockSpec(memory_space=pltpu.HBM)
    npair = NBLK // 2
    dma = pltpu.SemaphoreType.DMA
    vec = pltpu.VMEM((COLS, NBLK * LANES), F32)
    halo = pltpu.VMEM((3, COLS, REACH * LANES), F32)
    width = 4 * TILE
    return pl.pallas_call(
        functools.partial(filter_kernel, ntile, zc),
        out_shape=(
            jax.ShapeDtypeStruct((COLS, NBLK * TILE), F32),
            jax.ShapeDtypeStruct((NCOL * COLS, NCOL * COLS), F32),
        ),
        in_specs=[hbm, hbm, hbm, sm, hbm, sm, sm],
        out_specs=(vm, vm),
        scratch_shapes=[
            pltpu.VMEM((NBLK * 4 * 72, LANES), F32),
            pltpu.VMEM((NBLK, 4, TILE), jnp.int32),
            pltpu.VMEM((COLS, NBLK * TILE), F32),
            pltpu.VMEM((NBLK * TILE // LANES, LANES), F32),
            pltpu.VMEM((NBLK * 24, LANES), F32),
            pltpu.VMEM((NBLK * 24, 12 * LANES), F32),
            pltpu.VMEM((LANES, LANES), F32),
            pltpu.VMEM((LANES, LANES), F32),
            pltpu.VMEM((NBLK, LANES), F32),
            pltpu.VMEM((2, REACH, LANES, LANES), F32),
            pltpu.VMEM((npair + 2, 8 * LANES, 2 * LANES), BF16),
            pltpu.VMEM((npair + 2, 8 * LANES, 2 * LANES), BF16),
            vec, vec, vec,
            pltpu.VMEM((2, 2 * COLS, (NBLK + 2 * REACH) * LANES), BF16),
            halo, halo, halo,
            pltpu.VMEM((NCOL, NBLK // 4, COLS, width), F32),
            pltpu.VMEM((NBLK // 4, COLS, width), F32),
            pltpu.VMEM((8, share, LANES), F32),
            pltpu.VMEM((zc, share, LANES), F32),
            pltpu.VMEM((ny, share, LANES), F32),
            pltpu.VMEM((8 * NCOL, share, LANES), F32),
            pltpu.VMEM((NCOL * COLS, NCOL * COLS), F32),
            dma((4,)), dma((3,)), dma((3,)), dma((3,)), dma((3,)), dma((3,)),
            dma((18,)), dma((18,)), dma((3,)), dma((3,)),
        ],
        compiler_params=pltpu.CompilerParams(
            collective_id=0, has_side_effects=True, vmem_limit_bytes=57 * 1024 * 1024),
        name="filter",
    )(block, flat, intact, adjacency.T, diag, cut_low, cut_high)

def solution(mesh):
    in_specs = (
        P("col", "tile"),
        P("tile", None, None),
        P("tile", None, None),
        P("tile", None),
        P("tile"),
        P(),
        P(),
    )
    out_specs = (P("col", "tile"), P())
    return jax.shard_map(
        functools.partial(local, mesh.shape["tile"]), mesh=mesh, in_specs=in_specs, out_specs=out_specs,
        check_vma=False)
```

```python
import functools

import jax
import jax.numpy as jnp
from jax import lax
from jax.experimental import pallas as pl
from jax.experimental.pallas import tpu as pltpu
from jax.sharding import PartitionSpec as P

HIGH = lax.Precision.HIGHEST
TILE = 96
LANES = 128
NBLK = 24
REACH = 3
COLS = 32
NCOL = 4
MESH = pl.DeviceIdType.MESH
F32 = jnp.float32
BF16 = jnp.bfloat16


def aligned(x, step):
    return x if isinstance(x, int) else pl.multiple_of(x, step)


def roll(x, shift):
    return pltpu.roll(x, shift, 1)


def lane_id(rows):
    return lax.broadcasted_iota(jnp.int32, (rows, LANES), 1)


def spread_lanes(x0, x1, x2):
    lane = lane_id(x0.shape[0])
    b1 = jnp.where(lane < 32, roll(x0, 32), roll(x1, 32))
    b2 = jnp.where(lane < 64, roll(x1, 64), roll(x2, 64))
    return x0, b1, b2, roll(x2, 96)


def pack_lanes(b0, b1, b2, b3):
    lane = lane_id(b0.shape[0])
    x0 = jnp.where(lane < 96, b0, roll(b1, 96))
    x1 = jnp.where(lane < 64, roll(b1, 96), roll(b2, 64))
    x2 = jnp.where(lane < 32, roll(b2, 64), roll(b3, 32))
    return x0, x1, x2


def halves(x):
    hi = x.astype(BF16)
    return hi, (x - hi.astype(F32)).astype(BF16)


def contract(left, right, dims, precision=None):
    return lax.dot_general(left, right, (dims, ((), ())), precision=precision, preferred_element_type=F32)


def inverse_rows(a):
    groups = len(a)
    m = 8 * groups
    a = list(a)
    lane = lax.broadcasted_iota(jnp.int32, (8, m), 1)
    sub = lax.broadcasted_iota(jnp.int32, (8, m), 0)

    def every_row(x, t):
        return jnp.broadcast_to(x[t:t + 1], (8, m))

    def every_lane(x, k):
        return jnp.broadcast_to(x[:, k:k + 1], (8, m))

    out = []
    for g in range(groups):
        z = a[g]
        c = [every_lane(z, 8 * g + t) for t in range(8)]
        done = jnp.zeros((8, m), F32)
        pivots = jnp.ones((8, m), F32)
        for t in range(8):
            here = sub == t
            pivot = every_row(c[t], t)
            inv = 1.0 / pivot
            z = jnp.where(lane == 8 * g + t, jnp.where(here, 1.0, 0.0), z)
            row = every_row(z, t)
            done = jnp.where(here, row, done)
            pivots = jnp.where(here, pivot, pivots)
            row = row * inv
            fact = jnp.where(here, 0.0, c[t])
            z = jnp.where(here, row, z) - fact * row
            for u in range(t + 1, 8):
                same = every_row(c[u], t) * inv
                c[u] = jnp.where(here, same, c[u]) - fact * same
        rows = [every_row(z, t) for t in range(8)]
        panel = (lane >= 8 * g) & (lane < 8 * g + 8)
        for h in range(g + 1, groups):
            terms = [every_lane(a[h], 8 * g + t) * rows[t] for t in range(8)]
            total = ((terms[0] + terms[1]) + (terms[2] + terms[3])) + ((terms[4] + terms[5]) + (terms[6] + terms[7]))
            a[h] = jnp.where(panel, 0.0, a[h]) - total
        unit = jnp.where(lane < sub + 8 * g, done, jnp.where(lane == sub + 8 * g, 1.0, 0.0))
        out.append(unit / jnp.sqrt(pivots))
    return out


def ritz(col, hi_ref, lo_ref, sums_ref, high_ref, basis_ref, reduced_ref, inv_ref):
    groups = NCOL * COLS // 8
    rows = inverse_rows([sums_ref[8 * (g // 4) + g % 4] for g in range(groups)])
    for g in range(groups):
        inv_ref[8 * g:8 * g + 8, :] = rows[g]
    mine = inv_ref[pl.ds(col * COLS, COLS), :]
    mine = jnp.concatenate(halves(mine), axis=0)
    for g in range(NBLK // 4):
        hi, lo = (jnp.concatenate([ref[c, g] for c in range(NCOL)], axis=0) for ref in (hi_ref, lo_ref))
        width = hi.shape[1]
        both = contract(mine, hi, ((1,), (0,)))
        low = contract(mine[:COLS], lo, ((1,), (0,)))
        basis_ref[:, width * g:width * (g + 1)] = both[:COLS] + (both[COLS:] + low)

    def three(left, right, dims):
        both = contract(jnp.concatenate(left, axis=0), right[0], dims)
        rows = both.shape[0] // 2
        return both[:rows] + (both[rows:] + contract(left[0], right[1], dims))

    inverse = halves(inv_ref[...])
    proj = halves(jnp.concatenate([sums_ref[8 * (g // 4) + 4 + g % 4] for g in range(groups)], axis=0))
    half = halves(three(inverse, proj, ((1,), (0,))))
    reduced_ref[...] = three(half, inverse, ((1,), (1,))) / high_ref[0]


def filter_kernel(
    ntile, zc, block_ref, tiles_ref, intact_ref, adj_ref, diag_ref, low_ref, high_ref,
    basis_ref, reduced_ref,
    tiles_v, intact_v, block_v, diag_in, marks_k, marks_f, marks_in, marks_v, diag_v, merged, qh, qlo, v0, v1, v2, vh, ahead, spill, spill_out, dense, stiff,
    part, rx1, rx2, sums, inv_v, dense_hi, dense_lo,
    tile_sem, in_sem, ahead_send, ahead_recv, spill_send, spill_recv, x_send, x_recv, r_send, r_recv,
):
    tile = lax.axis_index("tile")
    col = lax.axis_index("col")
    ny = ntile // zc
    q = lax.rem(tile, zc)
    y = lax.div(tile, zc)
    following = lax.rem(tile + 1, ntile)
    previous = lax.rem(tile + ntile - 1, ntile)
    right = lax.rem(col + 1, NCOL)
    left = lax.rem(col + 3, NCOL)
    opposite = lax.rem(col + 2, NCOL)
    zpeers = [(y * zc + lax.rem(q + d, zc), col) for d in range(1, zc)]
    ypeers = [(lax.rem(y + d, ny) * zc + q, col) for d in range(1, ny)]
    core = lax.rem(q, 2)

    def near(dz, c, other):
        return (y * zc + lax.rem(q - core + 2 * dz + zc, zc) + (1 - core if other else core), c)

    spread = [near(dz, c, other) for c in (col, right, left, opposite) for dz in (0, 1, -1, -2)
              for other in (False, True)][1:]

    barrier = pltpu.get_barrier_semaphore()
    peers = [(following, col), (previous, col)] + ypeers + zpeers
    peers += [near(dz, c, other) for c in (right, left, opposite) for dz in (-2, -1, 0, 1, 2)
              for other in (False, True)]

    npair = NBLK // 2
    per = 4 * 72
    chunk = 3

    def tile_copy(i):
        rows = pl.ds(i * 2 * chunk * per, 2 * chunk * per)
        return pltpu.make_async_copy(tiles_ref.at[rows], tiles_v.at[rows], tile_sem.at[i])

    order = (3, 0, 1, 2)
    small = [pltpu.make_async_copy(src, dst, in_sem.at[i]) for i, (src, dst) in enumerate(
        ((intact_ref, intact_v), (block_ref, block_v), (diag_ref, diag_in)))]
    for copy in small:
        copy.start()
    for i in order:
        tile_copy(i).start()
    for peer in peers:
        pl.semaphore_signal(barrier, inc=1, device_id=peer, device_id_type=MESH)

    def window(buf, p, first=0, last=8):
        start = aligned(2 * LANES * p + LANES * first, LANES)
        return vh[buf, :, pl.ds(start, LANES * (last - first))]

    def keep(buf, p, value):
        hi, lo = halves(value)
        lanes = pl.ds(aligned(2 * LANES * p + REACH * LANES, LANES), value.shape[1])
        vh[buf, 0:COLS, lanes] = hi
        vh[buf, COLS:2 * COLS, lanes] = lo

    def pair(p):
        return pl.ds(aligned(2 * LANES * p, 2 * LANES), 2 * LANES)

    merged[...] = jnp.zeros(merged.shape, F32)
    for ref in (qh, qlo):
        for p, w, c in ((0, 0, 0), (0, 1, 0), (0, 2, 0), (0, 1, 1), (0, 2, 1), (1, 0, 0), (npair, 0, 1)):
            ref[p, pl.ds(LANES * w, LANES), pl.ds(LANES * c, LANES)] = jnp.zeros((LANES, LANES), BF16)
    for buf in range(2):
        vh[buf, :, 0:REACH * LANES] = jnp.zeros((2 * COLS, REACH * LANES), BF16)

    nmark = 3 * 4 * LANES
    rows_id = lax.broadcasted_iota(jnp.int32, (16, nmark), 0)
    lanes_id = lax.broadcasted_iota(jnp.int32, (16, nmark), 1)
    slot_at = lax.div(lanes_id, 3 * LANES)
    row_at = lax.div(lax.rem(lanes_id, 3 * LANES), TILE)
    pick = jnp.where(rows_id == 4 * row_at + slot_at, 1.0, 0.0).astype(BF16)
    marks_in[...] = jnp.zeros((LANES, LANES), F32)
    small[0].wait()
    for j in range(NBLK):
        marks_in[4 * j:4 * j + 4, 0:TILE] = intact_v[j].astype(F32)
    marks_v[...] = marks_in[...].T
    lane24 = lane_id(24)

    def gather_marks(j, _):
        total = jnp.zeros((24, LANES), F32)
        for rho in range(4):
            moved = roll(marks_v[pl.ds(rho, 24, stride=4), :], lax.rem(LANES + 4 * rho - 4 * j, LANES))
            total = jnp.where((lane24 >= 4 * rho) & (lane24 < 4 * rho + 4), moved, total)
        marks_k[pl.ds(pl.multiple_of(24 * j, 8), 24), :] = total
        return 0

    lax.fori_loop(0, NBLK, gather_marks, 0, unroll=4)

    def spread_marks(i, _):
        rows = pl.ds(pl.multiple_of(96 * i, 8), 96)
        marks_f[rows, :] = contract(marks_k[rows, 0:16].astype(BF16), pick, ((1,), (0,)))
        return 0

    lax.fori_loop(0, 6, spread_marks, 0, unroll=2)

    small[1].wait()
    valid32 = lane_id(COLS) < TILE
    for g in range(NBLK // 4):
        xs = [block_v[:, pl.ds((3 * g + i) * LANES, LANES)] for i in range(3)]
        for i, piece in enumerate(spread_lanes(*xs)):
            piece = jnp.where(valid32, piece, 0.0)
            v0[:, pl.ds((4 * g + i) * LANES, LANES)] = piece
            hi, lo = halves(piece)
            lanes = pl.ds((4 * g + i + REACH) * LANES, LANES)
            vh[0, 0:COLS, lanes] = hi
            vh[0, COLS:2 * COLS, lanes] = lo
    small[2].wait()
    xs = [diag_in[pl.ds(i, NBLK // 4, stride=3), :] for i in range(3)]
    for i, piece in enumerate(spread_lanes(*xs)):
        diag_v[pl.ds(i, NBLK // 4, stride=4), :] = piece

    pl.semaphore_wait(barrier, len(peers))

    def ahead_copy(a, vec):
        return pltpu.make_async_remote_copy(
            src_ref=vec.at[:, pl.ds(0, REACH * LANES)], dst_ref=ahead.at[a], send_sem=ahead_send.at[a],
            recv_sem=ahead_recv.at[a], device_id=(previous, col), device_id_type=MESH)

    ahead_copy(0, v0).start()

    valid24 = lane_id(24) < TILE

    def prepare(p):
        for par in range(2):
            j = 2 * p + par
            rows = pl.ds(24 * j, 24)
            slots = []
            for s in range(4):
                xs = [tiles_v[pl.ds(per * j + 4 * f + s, 24, stride=12), :] for f in range(3)]
                slots.append([x * marks_f[rows, pl.ds((3 * s + f) * LANES, LANES)] for f, x in enumerate(xs)])
            for r in range(REACH):
                here = [jnp.where(adj_ref[s, j] == r + 1, 1.0, 0.0).astype(F32) for s in range(4)]
                xs = []
                for f in range(3):
                    xs.append((slots[0][f] * here[0] + slots[1][f] * here[1])
                              + (slots[2][f] * here[2] + slots[3][f] * here[3]))
                for rho, piece in enumerate(spread_lanes(*xs)):
                    merged[par, r, pl.ds(rho, 24, stride=4), :] = jnp.where(valid24, piece, 0.0)
            for r in range(REACH):
                value = merged[par, r]
                target = par + r + 1
                back_rows = pl.ds(LANES * (par + 3 - 2 * (target // 2)), LANES)
                back_lanes = pl.ds(LANES * (target % 2), LANES)
                hi, lo = halves(value)
                qh[p + target // 2, back_rows, back_lanes] = hi
                qlo[p + target // 2, back_rows, back_lanes] = lo
                front_rows = pl.ds(LANES * (target + 3), LANES)
                hi, lo = halves(value.T)
                qh[p, front_rows, pl.ds(LANES * par, LANES)] = hi
                qlo[p, front_rows, pl.ds(LANES * par, LANES)] = lo
        for ref in (qh, qlo):
            for w, c in ((3, 0), (7, 0), (0, 1), (4, 1)):
                ref[p, pl.ds(LANES * w, LANES), pl.ds(LANES * c, LANES)] = jnp.zeros((LANES, LANES), BF16)

    has_next = tile < ntile - 1
    has_prev = tile > 0
    low = jnp.full((1, 2 * LANES), low_ref[0], F32)
    high = jnp.full((1, 2 * LANES), high_ref[0], F32)
    center = (low + high) / 2.0
    inv_half = 1.0 / ((high - low) / 2.0)

    def product(lhs, hi, lo):
        both = contract(lhs, hi, ((1,), (0,)))
        return both[:COLS] + both[COLS:] + contract(lhs[:COLS], lo, ((1,), (0,)))

    def couple(buf, p, first=0, last=8):
        rows = pl.ds(LANES * first, LANES * (last - first))
        return product(window(buf, p, first, last), qh[p, rows, :], qlo[p, rows, :])

    def spill_copy(a):
        return pltpu.make_async_remote_copy(
            src_ref=spill_out.at[a], dst_ref=spill.at[a], send_sem=spill_send.at[a],
            recv_sem=spill_recv.at[a], device_id=(following, col), device_id_type=MESH)

    def send_spill(a, buf):
        spill_out[a, :, 0:2 * LANES] = couple(buf, npair, 0, 3)
        tail = window(buf, npair, 1, 3)[:, LANES:2 * LANES]
        spill_out[a, :, 2 * LANES:3 * LANES] = product(
            tail, qh[npair + 1, 0:LANES, 0:LANES], qlo[npair + 1, 0:LANES, 0:LANES])
        spill_copy(a).start()

    def stiffness(vec, p, res):
        lanes = pair(p)
        d = jnp.concatenate([diag_v[pl.ds(2 * p, 1), :], diag_v[pl.ds(2 * p + 1, 1), :]], axis=1)
        return d * vec[:, lanes] - res

    def inside(buf, vec, finish, p):
        finish(p, stiffness(vec, p, couple(buf, p)))
        return 0

    def apply(a, buf, vec, finish, runs=((2, 10),), hook=None):
        for first, last in runs:
            lax.fori_loop(first, last, lambda p, _: inside(buf, vec, finish, p), 0, unroll=2)
            if hook is not None:
                hook(first // 2)
        heads = [couple(buf, p) for p in (0, 1)]
        tails = [couple(buf, npair - 2, 0, 6), couple(buf, npair - 1, 0, 4)]
        ahead_copy(a, vec).wait_recv()
        keep(buf, npair, jnp.where(has_next, ahead[a], 0.0))
        tails[0] += couple(buf, npair - 2, 6, 8)
        tails[1] += couple(buf, npair - 1, 4, 8)
        for i in range(2):
            finish(npair - 2 + i, stiffness(vec, npair - 2 + i, tails[i]))
        spill_copy(a).wait_recv()
        extra = jnp.where(has_prev, spill[a], 0.0)
        heads[0] += extra[:, 0:2 * LANES]
        heads[1] += jnp.concatenate([extra[:, 2 * LANES:], jnp.zeros((COLS, LANES), F32)], axis=1)
        for i in range(2):
            finish(i, stiffness(vec, i, heads[i]))
        ahead_copy(a, vec).wait_send()
        spill_copy(a).wait_send()

    def finish_first(p, kv):
        lanes = pair(p)
        value = (kv - center * v0[:, lanes]) * inv_half
        v1[:, lanes] = value
        keep(1, p, value)

    def finish_filtered(p, kv):
        lanes = pair(p)
        value = 2.0 * ((kv - center * v1[:, lanes]) * inv_half) - v0[:, lanes]
        v2[:, lanes] = value
        keep(0, p, value)

    def finish_stiff(p, kv):
        v1[:, pair(p)] = kv

    def compact(src, g):
        return pack_lanes(*[src[:, pl.ds((4 * g + k) * LANES, LANES)] for k in range(4)])

    ngroup = NBLK // 4
    lower = (0, 1, 2)
    upper = (3, 4, 5)

    def x_copy(i, source, g, to):
        return pltpu.make_async_remote_copy(
            src_ref=dense.at[source, g], dst_ref=dense.at[source, g], send_sem=x_send.at[i],
            recv_sem=x_recv.at[i], device_id=(tile, to), device_id_type=MESH)

    def to_right(g, source=None):
        if source is None:
            return x_copy(g, col, g, right)
        return x_copy(2 * ngroup + g, source, g, right)

    def to_left(g, source=None):
        if source is None:
            return x_copy(ngroup + g, col, g, left)
        return x_copy(2 * ngroup + g, source, g, left)

    def send_group(g):
        for i, x in enumerate(compact(v2, g)):
            dense[col, g, :, LANES * i:LANES * (i + 1)] = x
        to_right(g).start()
        to_left(g).start()

    def pass_on(g):
        if g in lower:
            to_right(g).wait_recv()
            to_right(g, left).start()
        else:
            to_left(g).wait_recv()
            to_left(g, right).start()

    def pass_on_pair(first):
        if first == 1:
            pass_on(2)
            pass_on(3)
        else:
            pass_on(0)
            pass_on(5)

    for n, i in enumerate(order):
        tile_copy(i).wait()
        for p in range(i * chunk, (i + 1) * chunk):
            prepare(p)
            if 2 < p < npair - chunk:
                inside(0, v0, finish_first, p - 1)
        if n == 0:
            send_spill(0, 0)
    apply(0, 0, v0, finish_first, ((npair - chunk - 1, npair - 2),))
    ahead_copy(1, v1).start()
    send_spill(1, 1)
    apply(1, 1, v1, finish_filtered, ((2, 4), (8, 10), (4, 6), (6, 8)), send_group)
    ahead_copy(2, v2).start()
    send_spill(2, 0)
    send_group(0)
    send_group(5)
    pass_on(1)
    pass_on(4)
    apply(2, 0, v2, finish_stiff, ((2, 6), (6, 10)), pass_on_pair)
    for g in range(ngroup):
        for i, x in enumerate(compact(v1, g)):
            stiff[g, :, LANES * i:LANES * (i + 1)] = x

    def split_rows(g):
        hi_f, lo_f = halves(dense[col, g])
        hi_s, lo_s = halves(stiff[g])
        return jnp.concatenate([hi_f, hi_s, lo_f, lo_s], axis=0)

    own = [split_rows(g) for g in range(ngroup)]

    def against(source, groups):
        lhs = jnp.concatenate([own[g] for g in groups], axis=1)
        parts = [halves(dense[source, g]) for g in groups]
        for g, (hi, lo) in zip(groups, parts):
            dense_hi[source, g] = hi
            dense_lo[source, g] = lo
        rhs = jnp.concatenate([jnp.concatenate([x[i] for x in parts], axis=1) for i in range(2)], axis=0)
        res = contract(lhs, rhs, ((1,), (1,)))
        half = 2 * COLS
        return res[:half, :COLS] + res[half:, :COLS] + (res[:half, COLS:] + res[half:, COLS:])

    mine = against(col, lower + upper)
    of_left = against(left, lower)
    of_right = against(right, upper)
    for g in upper:
        to_right(g).wait_recv()
    of_left += against(left, upper)
    for g in lower:
        to_left(g).wait_recv()
    of_right += against(right, lower)
    of_opposite = jnp.zeros((2 * COLS, COLS), F32)
    for groups in ((1, 2, 3, 4), (0, 5)):
        for g in groups:
            (to_right(g, left) if g in lower else to_left(g, right)).wait_recv()
        of_opposite += against(opposite, groups)
    total = jnp.concatenate([mine, of_right, of_opposite, of_left], axis=1)
    total = roll(total, COLS * col) * (1.0 / (NBLK * TILE * ntile))

    nshare = 8
    share = 2 * COLS // nshare
    for i in range(nshare):
        part[i] = total[share * i:share * (i + 1)]

    def r_copy(i, src, dst, to):
        return pltpu.make_async_remote_copy(
            src_ref=src, dst_ref=dst, send_sem=r_send.at[i], recv_sem=r_recv.at[i],
            device_id=to, device_id_type=MESH)

    def arrived(i, ref):
        copy = r_copy(i, ref, ref, (tile, right))
        copy.wait_recv()
        copy.wait_send()

    for d in range(1, zc):
        r_copy(0, part.at[lax.rem(q + d, nshare)], rx1.at[q], zpeers[d - 1]).start()
    own_share = lax.rem(q, nshare)
    rx1[q] = part[own_share]
    arrived(0, rx1.at[pl.ds(0, zc - 1)])
    mine = rx1[0]
    for i in range(1, zc):
        mine += rx1[i]
    rx2[y] = mine
    for peer in ypeers:
        r_copy(1, rx2.at[y], rx2.at[y], peer).start()
    arrived(1, rx2.at[pl.ds(0, ny - 1)])
    mine = rx2[0]
    for i in range(1, ny):
        mine += rx2[i]
    here = nshare * col + own_share
    sums[here] = mine
    for peer in spread:
        r_copy(2, sums.at[here], sums.at[here], peer).start()
    arrived(2, sums.at[pl.ds(0, NCOL * nshare - 1)])
    for g in range(ngroup):
        to_right(g).wait_send()
        to_left(g).wait_send()
        (to_right(g, left) if g in lower else to_left(g, right)).wait_send()
    ritz(col, dense_hi, dense_lo, sums, high_ref, basis_ref, reduced_ref, inv_v)


def hand_out_kernel(basis_in, reduced_in, basis_out, reduced_out, basis_v, reduced_v, in_sem, out_sem):
    parts = [(basis_in.at[pl.ds(8 * i, 8)], basis_v.at[pl.ds(8 * i, 8)], basis_out.at[pl.ds(8 * i, 8)])
             for i in range(COLS // 8)] + [(reduced_in, reduced_v, reduced_out)]
    there = [pltpu.make_async_copy(src, mid, in_sem.at[i]) for i, (src, mid, _) in enumerate(parts)]
    back = [pltpu.make_async_copy(mid, dst, out_sem.at[i]) for i, (_, mid, dst) in enumerate(parts)]
    for copy in there:
        copy.start()
    for first, second in zip(there, back):
        first.wait()
        second.start()
    for copy in back:
        copy.wait()


def local(ntile, block, tiles, intact, adjacency, stiff_diag, cut_low, cut_high):
    zc = min(16, ntile)
    ny = ntile // zc
    share = 2 * COLS // 8
    flat = tiles.reshape(NBLK, 4, 72, LANES).transpose(0, 2, 1, 3).reshape(NBLK * 4 * 72, LANES)
    diag = stiff_diag.reshape(NBLK * TILE // LANES, LANES)
    vm = pl.BlockSpec(memory_space=pltpu.VMEM)
    sm = pl.BlockSpec(memory_space=pltpu.SMEM)
    hbm = pl.BlockSpec(memory_space=pltpu.HBM)
    npair = NBLK // 2
    dma = pltpu.SemaphoreType.DMA
    vec = pltpu.VMEM((COLS, NBLK * LANES), F32)
    halo = pltpu.VMEM((3, COLS, REACH * LANES), F32)
    width = 4 * TILE
    basis, reduced = pl.pallas_call(
        functools.partial(filter_kernel, ntile, zc),
        out_shape=(
            jax.ShapeDtypeStruct((COLS, NBLK * TILE), F32),
            jax.ShapeDtypeStruct((NCOL * COLS, NCOL * COLS), F32),
        ),
        in_specs=[hbm, hbm, hbm, sm, hbm, sm, sm],
        out_specs=(vm, vm),
        scratch_shapes=[
            pltpu.VMEM((NBLK * 4 * 72, LANES), F32),
            pltpu.VMEM((NBLK, 4, TILE), jnp.int32),
            pltpu.VMEM((COLS, NBLK * TILE), F32),
            pltpu.VMEM((NBLK * TILE // LANES, LANES), F32),
            pltpu.VMEM((NBLK * 24, LANES), F32),
            pltpu.VMEM((NBLK * 24, 12 * LANES), F32),
            pltpu.VMEM((LANES, LANES), F32),
            pltpu.VMEM((LANES, LANES), F32),
            pltpu.VMEM((NBLK, LANES), F32),
            pltpu.VMEM((2, REACH, LANES, LANES), F32),
            pltpu.VMEM((npair + 2, 8 * LANES, 2 * LANES), BF16),
            pltpu.VMEM((npair + 2, 8 * LANES, 2 * LANES), BF16),
            vec, vec, vec,
            pltpu.VMEM((2, 2 * COLS, (NBLK + 2 * REACH) * LANES), BF16),
            halo, halo, halo,
            pltpu.VMEM((NCOL, NBLK // 4, COLS, width), F32),
            pltpu.VMEM((NBLK // 4, COLS, width), F32),
            pltpu.VMEM((8, share, LANES), F32),
            pltpu.VMEM((zc, share, LANES), F32),
            pltpu.VMEM((ny, share, LANES), F32),
            pltpu.VMEM((8 * NCOL, share, LANES), F32),
            pltpu.VMEM((NCOL * COLS, NCOL * COLS), F32),
            pltpu.VMEM((NCOL, NBLK // 4, COLS, width), BF16),
            pltpu.VMEM((NCOL, NBLK // 4, COLS, width), BF16),
            dma((4,)), dma((3,)), dma((3,)), dma((3,)), dma((3,)), dma((3,)),
            dma((18,)), dma((18,)), dma((3,)), dma((3,)),
        ],
        compiler_params=pltpu.CompilerParams(
            collective_id=0, has_side_effects=True, vmem_limit_bytes=57 * 1024 * 1024),
        name="filter",
    )(block, flat, intact, adjacency.T, diag, cut_low, cut_high)
    return pl.pallas_call(
        hand_out_kernel,
        out_shape=(
            jax.ShapeDtypeStruct((COLS, NBLK * TILE), F32),
            jax.ShapeDtypeStruct((NCOL * COLS, NCOL * COLS), F32),
        ),
        in_specs=[hbm, hbm],
        out_specs=(hbm, hbm),
        scratch_shapes=[
            pltpu.VMEM((COLS, NBLK * TILE), F32),
            pltpu.VMEM((NCOL * COLS, NCOL * COLS), F32),
            dma((5,)), dma((5,)),
        ],
        compiler_params=pltpu.CompilerParams(vmem_limit_bytes=57 * 1024 * 1024),
        name="hand_out",
    )(basis, reduced)


def solution(mesh):
    in_specs = (
        P("col", "tile"),
        P("tile", None, None),
        P("tile", None, None),
        P("tile", None),
        P("tile"),
        P(),
        P(),
    )
    out_specs = (P("col", "tile"), P())
    return jax.shard_map(
        functools.partial(local, mesh.shape["tile"]), mesh=mesh, in_specs=in_specs, out_specs=out_specs,
        check_vma=False)
```

```python
import functools

import jax
import jax.numpy as jnp
from jax import lax
from jax.experimental import pallas as pl
from jax.experimental.pallas import tpu as pltpu
from jax.sharding import PartitionSpec as P

HIGH = lax.Precision.HIGHEST
TILE = 96
LANES = 128
NBLK = 24
REACH = 3
COLS = 32
NCOL = 4
MESH = pl.DeviceIdType.MESH
F32 = jnp.float32
BF16 = jnp.bfloat16


def aligned(x, step):
    return x if isinstance(x, int) else pl.multiple_of(x, step)


def roll(x, shift):
    return pltpu.roll(x, shift, 1)


def lane_id(rows):
    return lax.broadcasted_iota(jnp.int32, (rows, LANES), 1)


def spread_lanes(x0, x1, x2):
    lane = lane_id(x0.shape[0])
    b1 = jnp.where(lane < 32, roll(x0, 32), roll(x1, 32))
    b2 = jnp.where(lane < 64, roll(x1, 64), roll(x2, 64))
    return x0, b1, b2, roll(x2, 96)


def pack_lanes(b0, b1, b2, b3):
    lane = lane_id(b0.shape[0])
    x0 = jnp.where(lane < 96, b0, roll(b1, 96))
    x1 = jnp.where(lane < 64, roll(b1, 96), roll(b2, 64))
    x2 = jnp.where(lane < 32, roll(b2, 64), roll(b3, 32))
    return x0, x1, x2


def halves(x):
    hi = x.astype(BF16)
    return hi, (x - hi.astype(F32)).astype(BF16)


def contract(left, right, dims, precision=None):
    return lax.dot_general(left, right, (dims, ((), ())), precision=precision, preferred_element_type=F32)


def inverse_rows(a):
    groups = len(a)
    m = 8 * groups
    a = list(a)
    lane = lax.broadcasted_iota(jnp.int32, (8, m), 1)
    sub = lax.broadcasted_iota(jnp.int32, (8, m), 0)
    pivots = []
    for g in range(groups):
        c = [[jnp.broadcast_to(a[h][:, 8 * g + t:8 * g + t + 1], (8, m)) for h in range(g, groups)] for t in range(8)]
        kept = jnp.ones((8, m), F32)
        for t in range(8):
            k = 8 * g + t
            pivot = jnp.broadcast_to(c[t][0][t:t + 1], (8, m))
            kept = jnp.where(sub == t, pivot, kept)
            inv = 1.0 / pivot
            row = jnp.where(lane == k, 1.0, jnp.broadcast_to(a[g][t:t + 1], (8, m)))
            facts = [x * inv for x in c[t]]
            facts[0] = jnp.where(sub > t, facts[0], 0.0)
            for u in range(t + 1, 8):
                same = jnp.broadcast_to(c[t][0][u:u + 1], (8, m))
                c[u] = [x - f * same for x, f in zip(c[u], facts)]
            for h in range(g, groups):
                old = jnp.where((lane == k) & (sub > t) if h == g else lane == k, 0.0, a[h])
                a[h] = old - facts[h - g] * row
        pivots.append(kept)
    out = []
    for g in range(groups):
        row = sub + 8 * g
        unit = jnp.where(lane < row, a[g], jnp.where(lane == row, 1.0, 0.0))
        out.append(unit / jnp.sqrt(pivots[g]))
    return out


def ritz(col, hi_ref, lo_ref, sums_ref, high_ref, basis_ref, reduced_ref, inv_ref):
    groups = NCOL * COLS // 8
    rows = inverse_rows([sums_ref[8 * (g // 4) + g % 4] for g in range(groups)])
    for g in range(groups):
        inv_ref[8 * g:8 * g + 8, :] = rows[g]
    mine = inv_ref[pl.ds(col * COLS, COLS), :]
    mine = jnp.concatenate(halves(mine), axis=0)
    for g in range(NBLK // 4):
        hi, lo = (jnp.concatenate([ref[c, g] for c in range(NCOL)], axis=0) for ref in (hi_ref, lo_ref))
        width = hi.shape[1]
        both = contract(mine, hi, ((1,), (0,)))
        low = contract(mine[:COLS], lo, ((1,), (0,)))
        basis_ref[:, width * g:width * (g + 1)] = both[:COLS] + (both[COLS:] + low)

    def three(left, right, dims):
        both = contract(jnp.concatenate(left, axis=0), right[0], dims)
        rows = both.shape[0] // 2
        return both[:rows] + (both[rows:] + contract(left[0], right[1], dims))

    inverse = halves(inv_ref[...])
    proj = halves(jnp.concatenate([sums_ref[8 * (g // 4) + 4 + g % 4] for g in range(groups)], axis=0))
    half = halves(three(inverse, proj, ((1,), (0,))))
    reduced_ref[...] = three(half, inverse, ((1,), (1,))) / high_ref[0]


def filter_kernel(
    ntile, zc, block_ref, tiles_ref, intact_ref, adj_ref, diag_ref, low_ref, high_ref,
    basis_ref, reduced_ref,
    tiles_v, intact_v, block_v, diag_in, marks_k, marks_f, marks_in, marks_v, diag_v, merged, qh, qlo, v0, v1, v2, vh, ahead, spill, spill_out, dense, stiff,
    part, rx1, rx2, sums, inv_v, dense_hi, dense_lo,
    tile_sem, in_sem, ahead_send, ahead_recv, spill_send, spill_recv, x_send, x_recv, r_send, r_recv,
):
    tile = lax.axis_index("tile")
    col = lax.axis_index("col")
    ny = ntile // zc
    q = lax.rem(tile, zc)
    y = lax.div(tile, zc)
    following = lax.rem(tile + 1, ntile)
    previous = lax.rem(tile + ntile - 1, ntile)
    right = lax.rem(col + 1, NCOL)
    left = lax.rem(col + 3, NCOL)
    opposite = lax.rem(col + 2, NCOL)
    zpeers = [(y * zc + lax.rem(q + d, zc), col) for d in range(1, zc)]
    ypeers = [(lax.rem(y + d, ny) * zc + q, col) for d in range(1, ny)]
    core = lax.rem(q, 2)

    def near(dz, c, other):
        return (y * zc + lax.rem(q - core + 2 * dz + zc, zc) + (1 - core if other else core), c)

    spread = [near(dz, c, other) for c in (col, right, left, opposite) for dz in (0, 1, -1, -2)
              for other in (False, True)][1:]

    barrier = pltpu.get_barrier_semaphore()
    peers = [(following, col), (previous, col)] + ypeers + zpeers
    peers += [near(dz, c, other) for c in (right, left, opposite) for dz in (-2, -1, 0, 1, 2)
              for other in (False, True)]

    npair = NBLK // 2
    per = 4 * 72
    chunk = 3

    def tile_copy(i):
        rows = pl.ds(i * 2 * chunk * per, 2 * chunk * per)
        return pltpu.make_async_copy(tiles_ref.at[rows], tiles_v.at[rows], tile_sem.at[i])

    order = (3, 0, 1, 2)
    small = [pltpu.make_async_copy(src, dst, in_sem.at[i]) for i, (src, dst) in enumerate(
        ((intact_ref, intact_v), (block_ref, block_v), (diag_ref, diag_in)))]
    for copy in small:
        copy.start()
    for i in order:
        tile_copy(i).start()
    for peer in peers:
        pl.semaphore_signal(barrier, inc=1, device_id=peer, device_id_type=MESH)

    def window(buf, p, first=0, last=8):
        start = aligned(2 * LANES * p + LANES * first, LANES)
        return vh[buf, :, pl.ds(start, LANES * (last - first))]

    def keep(buf, p, value):
        hi, lo = halves(value)
        lanes = pl.ds(aligned(2 * LANES * p + REACH * LANES, LANES), value.shape[1])
        vh[buf, 0:COLS, lanes] = hi
        vh[buf, COLS:2 * COLS, lanes] = lo

    def pair(p):
        return pl.ds(aligned(2 * LANES * p, 2 * LANES), 2 * LANES)

    merged[...] = jnp.zeros(merged.shape, F32)
    for ref in (qh, qlo):
        for p, w, c in ((0, 0, 0), (0, 1, 0), (0, 2, 0), (0, 1, 1), (0, 2, 1), (1, 0, 0), (npair, 0, 1)):
            ref[p, pl.ds(LANES * w, LANES), pl.ds(LANES * c, LANES)] = jnp.zeros((LANES, LANES), BF16)
    for buf in range(2):
        vh[buf, :, 0:REACH * LANES] = jnp.zeros((2 * COLS, REACH * LANES), BF16)

    nmark = 3 * 4 * LANES
    rows_id = lax.broadcasted_iota(jnp.int32, (16, nmark), 0)
    lanes_id = lax.broadcasted_iota(jnp.int32, (16, nmark), 1)
    slot_at = lax.div(lanes_id, 3 * LANES)
    row_at = lax.div(lax.rem(lanes_id, 3 * LANES), TILE)
    pick = jnp.where(rows_id == 4 * row_at + slot_at, 1.0, 0.0).astype(BF16)
    marks_in[...] = jnp.zeros((LANES, LANES), F32)
    small[0].wait()
    for j in range(NBLK):
        marks_in[4 * j:4 * j + 4, 0:TILE] = intact_v[j].astype(F32)
    marks_v[...] = marks_in[...].T
    lane24 = lane_id(24)

    def gather_marks(j, _):
        total = jnp.zeros((24, LANES), F32)
        for rho in range(4):
            moved = roll(marks_v[pl.ds(rho, 24, stride=4), :], lax.rem(LANES + 4 * rho - 4 * j, LANES))
            total = jnp.where((lane24 >= 4 * rho) & (lane24 < 4 * rho + 4), moved, total)
        marks_k[pl.ds(pl.multiple_of(24 * j, 8), 24), :] = total
        return 0

    lax.fori_loop(0, NBLK, gather_marks, 0, unroll=4)

    def spread_marks(i, _):
        rows = pl.ds(pl.multiple_of(96 * i, 8), 96)
        marks_f[rows, :] = contract(marks_k[rows, 0:16].astype(BF16), pick, ((1,), (0,)))
        return 0

    lax.fori_loop(0, 6, spread_marks, 0, unroll=2)

    small[1].wait()
    valid32 = lane_id(COLS) < TILE
    for g in range(NBLK // 4):
        xs = [block_v[:, pl.ds((3 * g + i) * LANES, LANES)] for i in range(3)]
        for i, piece in enumerate(spread_lanes(*xs)):
            piece = jnp.where(valid32, piece, 0.0)
            v0[:, pl.ds((4 * g + i) * LANES, LANES)] = piece
            hi, lo = halves(piece)
            lanes = pl.ds((4 * g + i + REACH) * LANES, LANES)
            vh[0, 0:COLS, lanes] = hi
            vh[0, COLS:2 * COLS, lanes] = lo
    small[2].wait()
    xs = [diag_in[pl.ds(i, NBLK // 4, stride=3), :] for i in range(3)]
    for i, piece in enumerate(spread_lanes(*xs)):
        diag_v[pl.ds(i, NBLK // 4, stride=4), :] = piece

    pl.semaphore_wait(barrier, len(peers))

    def ahead_copy(a, vec):
        return pltpu.make_async_remote_copy(
            src_ref=vec.at[:, pl.ds(0, REACH * LANES)], dst_ref=ahead.at[a], send_sem=ahead_send.at[a],
            recv_sem=ahead_recv.at[a], device_id=(previous, col), device_id_type=MESH)

    ahead_copy(0, v0).start()

    valid24 = lane_id(24) < TILE

    def prepare(p):
        for par in range(2):
            j = 2 * p + par
            rows = pl.ds(24 * j, 24)
            slots = []
            for s in range(4):
                xs = [tiles_v[pl.ds(per * j + 4 * f + s, 24, stride=12), :] for f in range(3)]
                slots.append([x * marks_f[rows, pl.ds((3 * s + f) * LANES, LANES)] for f, x in enumerate(xs)])
            for r in range(REACH):
                here = [jnp.where(adj_ref[s, j] == r + 1, 1.0, 0.0).astype(F32) for s in range(4)]
                xs = []
                for f in range(3):
                    xs.append((slots[0][f] * here[0] + slots[1][f] * here[1])
                              + (slots[2][f] * here[2] + slots[3][f] * here[3]))
                for rho, piece in enumerate(spread_lanes(*xs)):
                    merged[par, r, pl.ds(rho, 24, stride=4), :] = jnp.where(valid24, piece, 0.0)
            for r in range(REACH):
                value = merged[par, r]
                target = par + r + 1
                back_rows = pl.ds(LANES * (par + 3 - 2 * (target // 2)), LANES)
                back_lanes = pl.ds(LANES * (target % 2), LANES)
                hi, lo = halves(value)
                qh[p + target // 2, back_rows, back_lanes] = hi
                qlo[p + target // 2, back_rows, back_lanes] = lo
                front_rows = pl.ds(LANES * (target + 3), LANES)
                hi, lo = halves(value.T)
                qh[p, front_rows, pl.ds(LANES * par, LANES)] = hi
                qlo[p, front_rows, pl.ds(LANES * par, LANES)] = lo
        for ref in (qh, qlo):
            for w, c in ((3, 0), (7, 0), (0, 1), (4, 1)):
                ref[p, pl.ds(LANES * w, LANES), pl.ds(LANES * c, LANES)] = jnp.zeros((LANES, LANES), BF16)

    has_next = tile < ntile - 1
    has_prev = tile > 0
    low = jnp.full((1, 2 * LANES), low_ref[0], F32)
    high = jnp.full((1, 2 * LANES), high_ref[0], F32)
    center = (low + high) / 2.0
    inv_half = 1.0 / ((high - low) / 2.0)

    def product(lhs, hi, lo):
        both = contract(lhs, hi, ((1,), (0,)))
        return both[:COLS] + both[COLS:] + contract(lhs[:COLS], lo, ((1,), (0,)))

    def couple(buf, p, first=0, last=8):
        rows = pl.ds(LANES * first, LANES * (last - first))
        return product(window(buf, p, first, last), qh[p, rows, :], qlo[p, rows, :])

    def spill_copy(a):
        return pltpu.make_async_remote_copy(
            src_ref=spill_out.at[a], dst_ref=spill.at[a], send_sem=spill_send.at[a],
            recv_sem=spill_recv.at[a], device_id=(following, col), device_id_type=MESH)

    def send_spill(a, buf):
        spill_out[a, :, 0:2 * LANES] = couple(buf, npair, 0, 3)
        tail = window(buf, npair, 1, 3)[:, LANES:2 * LANES]
        spill_out[a, :, 2 * LANES:3 * LANES] = product(
            tail, qh[npair + 1, 0:LANES, 0:LANES], qlo[npair + 1, 0:LANES, 0:LANES])
        spill_copy(a).start()

    def stiffness(vec, p, res):
        lanes = pair(p)
        d = jnp.concatenate([diag_v[pl.ds(2 * p, 1), :], diag_v[pl.ds(2 * p + 1, 1), :]], axis=1)
        return d * vec[:, lanes] - res

    def inside(buf, vec, finish, p):
        finish(p, stiffness(vec, p, couple(buf, p)))
        return 0

    def run(buf, vec, finish, first, last):
        lax.fori_loop(first, last, lambda p, _: inside(buf, vec, finish, p), 0, unroll=2)

    def apply(a, buf, vec, finish, runs, hook=None, between=None):
        for first, last in runs:
            run(buf, vec, finish, first, last)
            if hook is not None:
                hook(first // 2)
        heads = [couple(buf, p) for p in (0, 1)]
        tails = [couple(buf, npair - 2, 0, 6), couple(buf, npair - 1, 0, 4)]
        if between is not None:
            between()
        ahead_copy(a, vec).wait_recv()
        keep(buf, npair, jnp.where(has_next, ahead[a], 0.0))
        tails[0] += couple(buf, npair - 2, 6, 8)
        tails[1] += couple(buf, npair - 1, 4, 8)
        for i in range(2):
            finish(npair - 2 + i, stiffness(vec, npair - 2 + i, tails[i]))
        spill_copy(a).wait_recv()
        extra = jnp.where(has_prev, spill[a], 0.0)
        heads[0] += extra[:, 0:2 * LANES]
        heads[1] += jnp.concatenate([extra[:, 2 * LANES:], jnp.zeros((COLS, LANES), F32)], axis=1)
        for i in range(2):
            finish(i, stiffness(vec, i, heads[i]))
        ahead_copy(a, vec).wait_send()
        spill_copy(a).wait_send()

    def finish_first(p, kv):
        lanes = pair(p)
        value = (kv - center * v0[:, lanes]) * inv_half
        v1[:, lanes] = value
        keep(1, p, value)

    def finish_filtered(p, kv):
        lanes = pair(p)
        value = 2.0 * ((kv - center * v1[:, lanes]) * inv_half) - v0[:, lanes]
        v2[:, lanes] = value
        keep(0, p, value)

    def finish_stiff(p, kv):
        v1[:, pair(p)] = kv

    def compact(src, g):
        return pack_lanes(*[src[:, pl.ds((4 * g + k) * LANES, LANES)] for k in range(4)])

    ngroup = NBLK // 4
    lower = (0, 1, 2)
    upper = (3, 4, 5)

    def x_copy(i, source, g, to):
        return pltpu.make_async_remote_copy(
            src_ref=dense.at[source, g], dst_ref=dense.at[source, g], send_sem=x_send.at[i],
            recv_sem=x_recv.at[i], device_id=(tile, to), device_id_type=MESH)

    def to_right(g, source=None):
        if source is None:
            return x_copy(g, col, g, right)
        return x_copy(2 * ngroup + g, source, g, right)

    def to_left(g, source=None):
        if source is None:
            return x_copy(ngroup + g, col, g, left)
        return x_copy(2 * ngroup + g, source, g, left)

    def send_group(g):
        for i, x in enumerate(compact(v2, g)):
            dense[col, g, :, LANES * i:LANES * (i + 1)] = x
        to_right(g).start()
        to_left(g).start()

    def pass_on(g):
        if g in lower:
            to_right(g).wait_recv()
            to_right(g, left).start()
        else:
            to_left(g).wait_recv()
            to_left(g, right).start()

    def start_second():
        for g in (2, 3):
            run(1, v1, finish_filtered, 2 * g, 2 * g + 2)
            send_group(g)

    def start_third():
        run(0, v2, finish_stiff, 4, 8)
        pass_on(2)
        pass_on(3)

    def last_relays(g):
        if g == 4:
            pass_on(0)
            pass_on(5)

    for n, i in enumerate(order):
        tile_copy(i).wait()
        for p in range(i * chunk, (i + 1) * chunk):
            prepare(p)
            if 2 < p < npair - chunk:
                inside(0, v0, finish_first, p - 1)
        if n == 0:
            send_spill(0, 0)
    apply(0, 0, v0, finish_first, ((npair - chunk - 1, npair - 2),), None, start_second)
    ahead_copy(1, v1).start()
    send_spill(1, 1)
    apply(1, 1, v1, finish_filtered, ((2, 4), (8, 10)), send_group, start_third)
    ahead_copy(2, v2).start()
    send_spill(2, 0)
    send_group(0)
    send_group(5)
    pass_on(1)
    pass_on(4)
    apply(2, 0, v2, finish_stiff, ((2, 4), (8, 10)), last_relays)
    for g in range(ngroup):
        for i, x in enumerate(compact(v1, g)):
            stiff[g, :, LANES * i:LANES * (i + 1)] = x

    def split_rows(g):
        hi_f, lo_f = halves(dense[col, g])
        hi_s, lo_s = halves(stiff[g])
        return jnp.concatenate([hi_f, hi_s, lo_f, lo_s], axis=0)

    own = [split_rows(g) for g in range(ngroup)]

    def against(source, groups):
        lhs = jnp.concatenate([own[g] for g in groups], axis=1)
        parts = [halves(dense[source, g]) for g in groups]
        for g, (hi, lo) in zip(groups, parts):
            dense_hi[source, g] = hi
            dense_lo[source, g] = lo
        rhs = jnp.concatenate([jnp.concatenate([x[i] for x in parts], axis=1) for i in range(2)], axis=0)
        res = contract(lhs, rhs, ((1,), (1,)))
        half = 2 * COLS
        return res[:half, :COLS] + res[half:, :COLS] + (res[:half, COLS:] + res[half:, COLS:])

    mine = against(col, lower + upper)
    of_left = against(left, lower)
    of_right = against(right, upper)
    for g in upper:
        to_right(g).wait_recv()
    of_left += against(left, upper)
    for g in lower:
        to_left(g).wait_recv()
    of_right += against(right, lower)
    of_opposite = jnp.zeros((2 * COLS, COLS), F32)
    for groups in ((1, 2, 3, 4), (0, 5)):
        for g in groups:
            (to_right(g, left) if g in lower else to_left(g, right)).wait_recv()
        of_opposite += against(opposite, groups)
    total = jnp.concatenate([mine, of_right, of_opposite, of_left], axis=1)
    total = roll(total, COLS * col) * (1.0 / (NBLK * TILE * ntile))

    nshare = 8
    share = 2 * COLS // nshare
    for i in range(nshare):
        part[i] = total[share * i:share * (i + 1)]

    def r_copy(i, src, dst, to):
        return pltpu.make_async_remote_copy(
            src_ref=src, dst_ref=dst, send_sem=r_send.at[i], recv_sem=r_recv.at[i],
            device_id=to, device_id_type=MESH)

    def arrived(i, ref):
        copy = r_copy(i, ref, ref, (tile, right))
        copy.wait_recv()
        copy.wait_send()

    for d in range(1, zc):
        r_copy(0, part.at[lax.rem(q + d, nshare)], rx1.at[q], zpeers[d - 1]).start()
    own_share = lax.rem(q, nshare)
    rx1[q] = part[own_share]
    arrived(0, rx1.at[pl.ds(0, zc - 1)])
    mine = rx1[0]
    for i in range(1, zc):
        mine += rx1[i]
    rx2[y] = mine
    for peer in ypeers:
        r_copy(1, rx2.at[y], rx2.at[y], peer).start()
    arrived(1, rx2.at[pl.ds(0, ny - 1)])
    mine = rx2[0]
    for i in range(1, ny):
        mine += rx2[i]
    here = nshare * col + own_share
    sums[here] = mine
    for peer in spread:
        r_copy(2, sums.at[here], sums.at[here], peer).start()
    arrived(2, sums.at[pl.ds(0, NCOL * nshare - 1)])
    for g in range(ngroup):
        to_right(g).wait_send()
        to_left(g).wait_send()
        (to_right(g, left) if g in lower else to_left(g, right)).wait_send()
    ritz(col, dense_hi, dense_lo, sums, high_ref, basis_ref, reduced_ref, inv_v)


def hand_out_kernel(basis_in, reduced_in, basis_out, reduced_out, basis_v, reduced_v, in_sem, out_sem):
    parts = [(basis_in.at[pl.ds(8 * i, 8)], basis_v.at[pl.ds(8 * i, 8)], basis_out.at[pl.ds(8 * i, 8)])
             for i in range(COLS // 8)] + [(reduced_in, reduced_v, reduced_out)]
    there = [pltpu.make_async_copy(src, mid, in_sem.at[i]) for i, (src, mid, _) in enumerate(parts)]
    back = [pltpu.make_async_copy(mid, dst, out_sem.at[i]) for i, (_, mid, dst) in enumerate(parts)]
    for copy in there:
        copy.start()
    for first, second in zip(there, back):
        first.wait()
        second.start()
    for copy in back:
        copy.wait()


def local(ntile, block, tiles, intact, adjacency, stiff_diag, cut_low, cut_high):
    zc = min(16, ntile)
    ny = ntile // zc
    share = 2 * COLS // 8
    flat = tiles.reshape(NBLK, 4, 72, LANES).transpose(0, 2, 1, 3).reshape(NBLK * 4 * 72, LANES)
    diag = stiff_diag.reshape(NBLK * TILE // LANES, LANES)
    vm = pl.BlockSpec(memory_space=pltpu.VMEM)
    sm = pl.BlockSpec(memory_space=pltpu.SMEM)
    hbm = pl.BlockSpec(memory_space=pltpu.HBM)
    npair = NBLK // 2
    dma = pltpu.SemaphoreType.DMA
    vec = pltpu.VMEM((COLS, NBLK * LANES), F32)
    halo = pltpu.VMEM((3, COLS, REACH * LANES), F32)
    width = 4 * TILE
    basis, reduced = pl.pallas_call(
        functools.partial(filter_kernel, ntile, zc),
        out_shape=(
            jax.ShapeDtypeStruct((COLS, NBLK * TILE), F32),
            jax.ShapeDtypeStruct((NCOL * COLS, NCOL * COLS), F32),
        ),
        in_specs=[hbm, hbm, hbm, sm, hbm, sm, sm],
        out_specs=(vm, vm),
        scratch_shapes=[
            pltpu.VMEM((NBLK * 4 * 72, LANES), F32),
            pltpu.VMEM((NBLK, 4, TILE), jnp.int32),
            pltpu.VMEM((COLS, NBLK * TILE), F32),
            pltpu.VMEM((NBLK * TILE // LANES, LANES), F32),
            pltpu.VMEM((NBLK * 24, LANES), F32),
            pltpu.VMEM((NBLK * 24, 12 * LANES), F32),
            pltpu.VMEM((LANES, LANES), F32),
            pltpu.VMEM((LANES, LANES), F32),
            pltpu.VMEM((NBLK, LANES), F32),
            pltpu.VMEM((2, REACH, LANES, LANES), F32),
            pltpu.VMEM((npair + 2, 8 * LANES, 2 * LANES), BF16),
            pltpu.VMEM((npair + 2, 8 * LANES, 2 * LANES), BF16),
            vec, vec, vec,
            pltpu.VMEM((2, 2 * COLS, (NBLK + 2 * REACH) * LANES), BF16),
            halo, halo, halo,
            pltpu.VMEM((NCOL, NBLK // 4, COLS, width), F32),
            pltpu.VMEM((NBLK // 4, COLS, width), F32),
            pltpu.VMEM((8, share, LANES), F32),
            pltpu.VMEM((zc, share, LANES), F32),
            pltpu.VMEM((ny, share, LANES), F32),
            pltpu.VMEM((8 * NCOL, share, LANES), F32),
            pltpu.VMEM((NCOL * COLS, NCOL * COLS), F32),
            pltpu.VMEM((NCOL, NBLK // 4, COLS, width), BF16),
            pltpu.VMEM((NCOL, NBLK // 4, COLS, width), BF16),
            dma((4,)), dma((3,)), dma((3,)), dma((3,)), dma((3,)), dma((3,)),
            dma((18,)), dma((18,)), dma((3,)), dma((3,)),
        ],
        compiler_params=pltpu.CompilerParams(
            collective_id=0, has_side_effects=True, vmem_limit_bytes=57 * 1024 * 1024),
        name="filter",
    )(block, flat, intact, adjacency.T, diag, cut_low, cut_high)
    return pl.pallas_call(
        hand_out_kernel,
        out_shape=(
            jax.ShapeDtypeStruct((COLS, NBLK * TILE), F32),
            jax.ShapeDtypeStruct((NCOL * COLS, NCOL * COLS), F32),
        ),
        in_specs=[hbm, hbm],
        out_specs=(hbm, hbm),
        scratch_shapes=[
            pltpu.VMEM((COLS, NBLK * TILE), F32),
            pltpu.VMEM((NCOL * COLS, NCOL * COLS), F32),
            dma((5,)), dma((5,)),
        ],
        compiler_params=pltpu.CompilerParams(vmem_limit_bytes=57 * 1024 * 1024),
        name="hand_out",
    )(basis, reduced)


def solution(mesh):
    in_specs = (
        P("col", "tile"),
        P("tile", None, None),
        P("tile", None, None),
        P("tile", None),
        P("tile"),
        P(),
        P(),
    )
    out_specs = (P("col", "tile"), P())
    return jax.shard_map(
        functools.partial(local, mesh.shape["tile"]), mesh=mesh, in_specs=in_specs, out_specs=out_specs,
        check_vma=False)
```

```python
import functools

import jax
import jax.numpy as jnp
from jax import lax
from jax.experimental import pallas as pl
from jax.experimental.pallas import tpu as pltpu
from jax.sharding import PartitionSpec as P

HIGH = lax.Precision.HIGHEST
TILE = 96
LANES = 128
NBLK = 24
REACH = 3
COLS = 32
NCOL = 4
MESH = pl.DeviceIdType.MESH
F32 = jnp.float32
BF16 = jnp.bfloat16


def aligned(x, step):
    return x if isinstance(x, int) else pl.multiple_of(x, step)


def roll(x, shift):
    return pltpu.roll(x, shift, 1)


def lane_id(rows):
    return lax.broadcasted_iota(jnp.int32, (rows, LANES), 1)


def spread_lanes(x0, x1, x2):
    lane = lane_id(x0.shape[0])
    b1 = jnp.where(lane < 32, roll(x0, 32), roll(x1, 32))
    b2 = jnp.where(lane < 64, roll(x1, 64), roll(x2, 64))
    return x0, b1, b2, roll(x2, 96)


def pack_lanes(b0, b1, b2, b3):
    lane = lane_id(b0.shape[0])
    x0 = jnp.where(lane < 96, b0, roll(b1, 96))
    x1 = jnp.where(lane < 64, roll(b1, 96), roll(b2, 64))
    x2 = jnp.where(lane < 32, roll(b2, 64), roll(b3, 32))
    return x0, x1, x2


def halves(x):
    hi = x.astype(BF16)
    return hi, (x - hi.astype(F32)).astype(BF16)


def contract(left, right, dims, precision=None):
    return lax.dot_general(left, right, (dims, ((), ())), precision=precision, preferred_element_type=F32)


def inverse_rows(a):
    groups = len(a)
    m = 8 * groups
    a = list(a)
    lane = lax.broadcasted_iota(jnp.int32, (8, m), 1)
    sub = lax.broadcasted_iota(jnp.int32, (8, m), 0)
    pivots = []
    for g in range(groups):
        c = [[jnp.broadcast_to(a[h][:, 8 * g + t:8 * g + t + 1], (8, m)) for h in range(g, groups)] for t in range(8)]
        kept = jnp.ones((8, m), F32)
        for t in range(8):
            k = 8 * g + t
            pivot = jnp.broadcast_to(c[t][0][t:t + 1], (8, m))
            kept = jnp.where(sub == t, pivot, kept)
            inv = 1.0 / pivot
            row = jnp.where(lane == k, 1.0, jnp.broadcast_to(a[g][t:t + 1], (8, m)))
            facts = [x * inv for x in c[t]]
            facts[0] = jnp.where(sub > t, facts[0], 0.0)
            for u in range(t + 1, 8):
                same = jnp.broadcast_to(c[t][0][u:u + 1], (8, m))
                c[u] = [x - f * same for x, f in zip(c[u], facts)]
            for h in range(g, groups):
                old = jnp.where((lane == k) & (sub > t) if h == g else lane == k, 0.0, a[h])
                a[h] = old - facts[h - g] * row
        pivots.append(kept)
    out = []
    for g in range(groups):
        row = sub + 8 * g
        unit = jnp.where(lane < row, a[g], jnp.where(lane == row, 1.0, 0.0))
        out.append(unit / jnp.sqrt(pivots[g]))
    return out


def ritz(col, hi_ref, lo_ref, sums_ref, high_ref, basis_ref, reduced_ref, inv_ref, outs):
    groups = NCOL * COLS // 8
    rows = inverse_rows([sums_ref[8 * (g // 4) + g % 4] for g in range(groups)])
    for g in range(groups):
        inv_ref[8 * g:8 * g + 8, :] = rows[g]
    mine = inv_ref[pl.ds(col * COLS, COLS), :]
    mine = jnp.concatenate(halves(mine), axis=0)
    for g in range(NBLK // 4):
        hi, lo = (jnp.concatenate([ref[c, g] for c in range(NCOL)], axis=0) for ref in (hi_ref, lo_ref))
        width = hi.shape[1]
        both = contract(mine, hi, ((1,), (0,)))
        low = contract(mine[:COLS], lo, ((1,), (0,)))
        basis_ref[:, width * g:width * (g + 1)] = both[:COLS] + (both[COLS:] + low)

    outs[0].start()

    def three(left, right, dims):
        both = contract(jnp.concatenate(left, axis=0), right[0], dims)
        rows = both.shape[0] // 2
        return both[:rows] + (both[rows:] + contract(left[0], right[1], dims))

    inverse = halves(inv_ref[...])
    proj = halves(jnp.concatenate([sums_ref[8 * (g // 4) + 4 + g % 4] for g in range(groups)], axis=0))
    half = halves(three(inverse, proj, ((1,), (0,))))
    reduced_ref[...] = three(half, inverse, ((1,), (1,))) / high_ref[0]
    outs[1].start()


def filter_kernel(
    ntile, zc, block_ref, tiles_ref, intact_ref, adj_hbm, diag_ref, low_hbm, high_hbm,
    basis_out, reduced_out,
    adj_ref, low_ref, high_ref, basis_v, reduced_v, tiles_v, intact_v, block_v, diag_in, marks_k, marks_f, marks_in, marks_v, diag_v, merged, qh, qlo, v0, v1, v2, vh, ahead, spill, spill_out, dense, stiff,
    part, rx1, rx2, sums, inv_v, dense_hi, dense_lo,
    tile_sem, in_sem, out_sem, ahead_send, ahead_recv, spill_send, spill_recv, x_send, x_recv, r_send, r_recv,
):
    tile = lax.axis_index("tile")
    col = lax.axis_index("col")
    ny = ntile // zc
    q = lax.rem(tile, zc)
    y = lax.div(tile, zc)
    following = lax.rem(tile + 1, ntile)
    previous = lax.rem(tile + ntile - 1, ntile)
    right = lax.rem(col + 1, NCOL)
    left = lax.rem(col + 3, NCOL)
    opposite = lax.rem(col + 2, NCOL)
    zpeers = [(y * zc + lax.rem(q + d, zc), col) for d in range(1, zc)]
    ypeers = [(lax.rem(y + d, ny) * zc + q, col) for d in range(1, ny)]
    core = lax.rem(q, 2)

    def near(dz, c, other):
        return (y * zc + lax.rem(q - core + 2 * dz + zc, zc) + (1 - core if other else core), c)

    spread = [near(dz, c, other) for c in (col, right, left, opposite) for dz in (0, 1, -1, -2)
              for other in (False, True)][1:]

    barrier = pltpu.get_barrier_semaphore()
    peers = [(following, col), (previous, col)] + ypeers + zpeers
    peers += [near(dz, c, other) for c in (right, left, opposite) for dz in (-2, -1, 0, 1, 2)
              for other in (False, True)]

    npair = NBLK // 2
    per = 4 * 72
    chunk = 3

    def tile_copy(i):
        rows = pl.ds(i * 2 * chunk * per, 2 * chunk * per)
        return pltpu.make_async_copy(tiles_ref.at[rows], tiles_v.at[rows], tile_sem.at[i])

    order = (3, 0, 1, 2)
    small = [pltpu.make_async_copy(src, dst, in_sem.at[i]) for i, (src, dst) in enumerate(
        ((intact_ref, intact_v), (block_ref, block_v), (diag_ref, diag_in), (adj_hbm, adj_ref), (low_hbm, low_ref),
         (high_hbm, high_ref)))]
    for copy in small:
        copy.start()
    for i in order:
        tile_copy(i).start()
    for peer in peers:
        pl.semaphore_signal(barrier, inc=1, device_id=peer, device_id_type=MESH)

    def window(buf, p, first=0, last=8):
        start = aligned(2 * LANES * p + LANES * first, LANES)
        return vh[buf, :, pl.ds(start, LANES * (last - first))]

    def keep(buf, p, value):
        hi, lo = halves(value)
        lanes = pl.ds(aligned(2 * LANES * p + REACH * LANES, LANES), value.shape[1])
        vh[buf, 0:COLS, lanes] = hi
        vh[buf, COLS:2 * COLS, lanes] = lo

    def pair(p):
        return pl.ds(aligned(2 * LANES * p, 2 * LANES), 2 * LANES)

    merged[...] = jnp.zeros(merged.shape, F32)
    for ref in (qh, qlo):
        for p, w, c in ((0, 0, 0), (0, 1, 0), (0, 2, 0), (0, 1, 1), (0, 2, 1), (1, 0, 0), (npair, 0, 1)):
            ref[p, pl.ds(LANES * w, LANES), pl.ds(LANES * c, LANES)] = jnp.zeros((LANES, LANES), BF16)
    for buf in range(2):
        vh[buf, :, 0:REACH * LANES] = jnp.zeros((2 * COLS, REACH * LANES), BF16)

    nmark = 3 * 4 * LANES
    rows_id = lax.broadcasted_iota(jnp.int32, (16, nmark), 0)
    lanes_id = lax.broadcasted_iota(jnp.int32, (16, nmark), 1)
    slot_at = lax.div(lanes_id, 3 * LANES)
    row_at = lax.div(lax.rem(lanes_id, 3 * LANES), TILE)
    pick = jnp.where(rows_id == 4 * row_at + slot_at, 1.0, 0.0).astype(BF16)
    marks_in[...] = jnp.zeros((LANES, LANES), F32)
    small[0].wait()
    for j in range(NBLK):
        marks_in[4 * j:4 * j + 4, 0:TILE] = intact_v[j].astype(F32)
    marks_v[...] = marks_in[...].T
    lane24 = lane_id(24)

    def gather_marks(j, _):
        total = jnp.zeros((24, LANES), F32)
        for rho in range(4):
            moved = roll(marks_v[pl.ds(rho, 24, stride=4), :], lax.rem(LANES + 4 * rho - 4 * j, LANES))
            total = jnp.where((lane24 >= 4 * rho) & (lane24 < 4 * rho + 4), moved, total)
        marks_k[pl.ds(pl.multiple_of(24 * j, 8), 24), :] = total
        return 0

    lax.fori_loop(0, NBLK, gather_marks, 0, unroll=4)

    def spread_marks(i, _):
        rows = pl.ds(pl.multiple_of(96 * i, 8), 96)
        marks_f[rows, :] = contract(marks_k[rows, 0:16].astype(BF16), pick, ((1,), (0,)))
        return 0

    lax.fori_loop(4, 6, spread_marks, 0, unroll=2)

    small[1].wait()
    valid32 = lane_id(COLS) < TILE
    for g in range(NBLK // 4):
        xs = [block_v[:, pl.ds((3 * g + i) * LANES, LANES)] for i in range(3)]
        for i, piece in enumerate(spread_lanes(*xs)):
            piece = jnp.where(valid32, piece, 0.0)
            v0[:, pl.ds((4 * g + i) * LANES, LANES)] = piece
            hi, lo = halves(piece)
            lanes = pl.ds((4 * g + i + REACH) * LANES, LANES)
            vh[0, 0:COLS, lanes] = hi
            vh[0, COLS:2 * COLS, lanes] = lo
    for copy in small[2:]:
        copy.wait()
    xs = [diag_in[pl.ds(i, NBLK // 4, stride=3), :] for i in range(3)]
    for i, piece in enumerate(spread_lanes(*xs)):
        diag_v[pl.ds(i, NBLK // 4, stride=4), :] = piece

    pl.semaphore_wait(barrier, len(peers))

    def ahead_copy(a, vec):
        return pltpu.make_async_remote_copy(
            src_ref=vec.at[:, pl.ds(0, REACH * LANES)], dst_ref=ahead.at[a], send_sem=ahead_send.at[a],
            recv_sem=ahead_recv.at[a], device_id=(previous, col), device_id_type=MESH)

    ahead_copy(0, v0).start()

    valid24 = lane_id(24) < TILE

    def prepare(p):
        for par in range(2):
            j = 2 * p + par
            rows = pl.ds(24 * j, 24)
            slots = []
            for s in range(4):
                xs = [tiles_v[pl.ds(per * j + 4 * f + s, 24, stride=12), :] for f in range(3)]
                slots.append([x * marks_f[rows, pl.ds((3 * s + f) * LANES, LANES)] for f, x in enumerate(xs)])
            for r in range(REACH):
                here = [jnp.where(adj_ref[s, j] == r + 1, 1.0, 0.0).astype(F32) for s in range(4)]
                xs = []
                for f in range(3):
                    xs.append((slots[0][f] * here[0] + slots[1][f] * here[1])
                              + (slots[2][f] * here[2] + slots[3][f] * here[3]))
                for rho, piece in enumerate(spread_lanes(*xs)):
                    merged[par, r, pl.ds(rho, 24, stride=4), :] = jnp.where(valid24, piece, 0.0)
            for r in range(REACH):
                value = merged[par, r]
                target = par + r + 1
                back_rows = pl.ds(LANES * (par + 3 - 2 * (target // 2)), LANES)
                back_lanes = pl.ds(LANES * (target % 2), LANES)
                hi, lo = halves(value)
                qh[p + target // 2, back_rows, back_lanes] = hi
                qlo[p + target // 2, back_rows, back_lanes] = lo
                front_rows = pl.ds(LANES * (target + 3), LANES)
                hi, lo = halves(value.T)
                qh[p, front_rows, pl.ds(LANES * par, LANES)] = hi
                qlo[p, front_rows, pl.ds(LANES * par, LANES)] = lo
        for ref in (qh, qlo):
            for w, c in ((3, 0), (7, 0), (0, 1), (4, 1)):
                ref[p, pl.ds(LANES * w, LANES), pl.ds(LANES * c, LANES)] = jnp.zeros((LANES, LANES), BF16)

    has_next = tile < ntile - 1
    has_prev = tile > 0
    low = jnp.full((1, 2 * LANES), low_ref[0], F32)
    high = jnp.full((1, 2 * LANES), high_ref[0], F32)
    center = (low + high) / 2.0
    inv_half = 1.0 / ((high - low) / 2.0)

    def product(lhs, hi, lo):
        both = contract(lhs, hi, ((1,), (0,)))
        return both[:COLS] + both[COLS:] + contract(lhs[:COLS], lo, ((1,), (0,)))

    def couple(buf, p, first=0, last=8):
        rows = pl.ds(LANES * first, LANES * (last - first))
        return product(window(buf, p, first, last), qh[p, rows, :], qlo[p, rows, :])

    def spill_copy(a):
        return pltpu.make_async_remote_copy(
            src_ref=spill_out.at[a], dst_ref=spill.at[a], send_sem=spill_send.at[a],
            recv_sem=spill_recv.at[a], device_id=(following, col), device_id_type=MESH)

    def send_spill(a, buf):
        spill_out[a, :, 0:2 * LANES] = couple(buf, npair, 0, 3)
        tail = window(buf, npair, 1, 3)[:, LANES:2 * LANES]
        spill_out[a, :, 2 * LANES:3 * LANES] = product(
            tail, qh[npair + 1, 0:LANES, 0:LANES], qlo[npair + 1, 0:LANES, 0:LANES])
        spill_copy(a).start()

    def stiffness(vec, p, res):
        lanes = pair(p)
        d = jnp.concatenate([diag_v[pl.ds(2 * p, 1), :], diag_v[pl.ds(2 * p + 1, 1), :]], axis=1)
        return d * vec[:, lanes] - res

    def inside(buf, vec, finish, p):
        finish(p, stiffness(vec, p, couple(buf, p)))
        return 0

    def run(buf, vec, finish, first, last):
        lax.fori_loop(first, last, lambda p, _: inside(buf, vec, finish, p), 0, unroll=2)

    def apply(a, buf, vec, finish, runs, hook=None, between=None):
        for first, last in runs:
            run(buf, vec, finish, first, last)
            if hook is not None:
                hook(first // 2)
        heads = [couple(buf, p) for p in (0, 1)]
        tails = [couple(buf, npair - 2, 0, 6), couple(buf, npair - 1, 0, 4)]
        if between is not None:
            between()
        ahead_copy(a, vec).wait_recv()
        keep(buf, npair, jnp.where(has_next, ahead[a], 0.0))
        tails[0] += couple(buf, npair - 2, 6, 8)
        tails[1] += couple(buf, npair - 1, 4, 8)
        for i in range(2):
            finish(npair - 2 + i, stiffness(vec, npair - 2 + i, tails[i]))
        spill_copy(a).wait_recv()
        extra = jnp.where(has_prev, spill[a], 0.0)
        heads[0] += extra[:, 0:2 * LANES]
        heads[1] += jnp.concatenate([extra[:, 2 * LANES:], jnp.zeros((COLS, LANES), F32)], axis=1)
        for i in range(2):
            finish(i, stiffness(vec, i, heads[i]))
        ahead_copy(a, vec).wait_send()
        spill_copy(a).wait_send()

    def finish_first(p, kv):
        lanes = pair(p)
        value = (kv - center * v0[:, lanes]) * inv_half
        v1[:, lanes] = value
        keep(1, p, value)

    def finish_filtered(p, kv):
        lanes = pair(p)
        value = 2.0 * ((kv - center * v1[:, lanes]) * inv_half) - v0[:, lanes]
        v2[:, lanes] = value
        keep(0, p, value)

    def finish_stiff(p, kv):
        v1[:, pair(p)] = kv

    def compact(src, g):
        return pack_lanes(*[src[:, pl.ds((4 * g + k) * LANES, LANES)] for k in range(4)])

    ngroup = NBLK // 4
    lower = (0, 1, 2)
    upper = (3, 4, 5)

    def x_copy(i, source, g, to):
        return pltpu.make_async_remote_copy(
            src_ref=dense.at[source, g], dst_ref=dense.at[source, g], send_sem=x_send.at[i],
            recv_sem=x_recv.at[i], device_id=(tile, to), device_id_type=MESH)

    def to_right(g, source=None):
        if source is None:
            return x_copy(g, col, g, right)
        return x_copy(2 * ngroup + g, source, g, right)

    def to_left(g, source=None):
        if source is None:
            return x_copy(ngroup + g, col, g, left)
        return x_copy(2 * ngroup + g, source, g, left)

    def send_group(g):
        for i, x in enumerate(compact(v2, g)):
            dense[col, g, :, LANES * i:LANES * (i + 1)] = x
        to_right(g).start()
        to_left(g).start()

    def pass_on(g):
        if g in lower:
            to_right(g).wait_recv()
            to_right(g, left).start()
        else:
            to_left(g).wait_recv()
            to_left(g, right).start()

    def start_second():
        for g in (2, 3):
            run(1, v1, finish_filtered, 2 * g, 2 * g + 2)
            send_group(g)

    def start_third():
        run(0, v2, finish_stiff, 4, 8)
        pass_on(2)
        pass_on(3)

    def last_relays(g):
        if g == 4:
            pass_on(0)
            pass_on(5)

    for n, i in enumerate(order):
        tile_copy(i).wait()
        for p in range(i * chunk, (i + 1) * chunk):
            prepare(p)
            if 2 < p < npair - chunk:
                inside(0, v0, finish_first, p - 1)
        if n == 0:
            send_spill(0, 0)
            lax.fori_loop(0, 4, spread_marks, 0, unroll=2)
    apply(0, 0, v0, finish_first, ((npair - chunk - 1, npair - 2),), None, start_second)
    ahead_copy(1, v1).start()
    send_spill(1, 1)
    apply(1, 1, v1, finish_filtered, ((2, 4), (8, 10)), send_group, start_third)
    ahead_copy(2, v2).start()
    send_spill(2, 0)
    send_group(0)
    send_group(5)
    pass_on(1)
    pass_on(4)
    apply(2, 0, v2, finish_stiff, ((2, 4), (8, 10)), last_relays)
    for g in range(ngroup):
        for i, x in enumerate(compact(v1, g)):
            stiff[g, :, LANES * i:LANES * (i + 1)] = x

    def split_rows(g):
        hi_f, lo_f = halves(dense[col, g])
        hi_s, lo_s = halves(stiff[g])
        return jnp.concatenate([hi_f, hi_s, lo_f, lo_s], axis=0)

    own = [split_rows(g) for g in range(ngroup)]

    def against(source, groups):
        lhs = jnp.concatenate([own[g] for g in groups], axis=1)
        parts = [halves(dense[source, g]) for g in groups]
        for g, (hi, lo) in zip(groups, parts):
            dense_hi[source, g] = hi
            dense_lo[source, g] = lo
        rhs = jnp.concatenate([jnp.concatenate([x[i] for x in parts], axis=1) for i in range(2)], axis=0)
        res = contract(lhs, rhs, ((1,), (1,)))
        half = 2 * COLS
        return res[:half, :COLS] + res[half:, :COLS] + (res[:half, COLS:] + res[half:, COLS:])

    mine = against(col, lower + upper)
    of_left = against(left, lower)
    of_right = against(right, upper)
    for g in upper:
        to_right(g).wait_recv()
    of_left += against(left, upper)
    for g in lower:
        to_left(g).wait_recv()
    of_right += against(right, lower)
    of_opposite = jnp.zeros((2 * COLS, COLS), F32)
    for groups in ((1, 2, 3, 4), (0, 5)):
        for g in groups:
            (to_right(g, left) if g in lower else to_left(g, right)).wait_recv()
        of_opposite += against(opposite, groups)
    total = jnp.concatenate([mine, of_right, of_opposite, of_left], axis=1)
    total = roll(total, COLS * col) * (1.0 / (NBLK * TILE * ntile))

    nshare = 8
    share = 2 * COLS // nshare
    for i in range(nshare):
        part[i] = total[share * i:share * (i + 1)]

    def r_copy(i, src, dst, to):
        return pltpu.make_async_remote_copy(
            src_ref=src, dst_ref=dst, send_sem=r_send.at[i], recv_sem=r_recv.at[i],
            device_id=to, device_id_type=MESH)

    def arrived(i, ref):
        copy = r_copy(i, ref, ref, (tile, right))
        copy.wait_recv()
        copy.wait_send()

    for d in range(1, zc):
        r_copy(0, part.at[lax.rem(q + d, nshare)], rx1.at[q], zpeers[d - 1]).start()
    own_share = lax.rem(q, nshare)
    rx1[q] = part[own_share]
    arrived(0, rx1.at[pl.ds(0, zc - 1)])
    mine = rx1[0]
    for i in range(1, zc):
        mine += rx1[i]
    rx2[y] = mine
    for peer in ypeers:
        r_copy(1, rx2.at[y], rx2.at[y], peer).start()
    arrived(1, rx2.at[pl.ds(0, ny - 1)])
    mine = rx2[0]
    for i in range(1, ny):
        mine += rx2[i]
    here = nshare * col + own_share
    sums[here] = mine
    for peer in spread:
        r_copy(2, sums.at[here], sums.at[here], peer).start()
    arrived(2, sums.at[pl.ds(0, NCOL * nshare - 1)])
    for g in range(ngroup):
        to_right(g).wait_send()
        to_left(g).wait_send()
        (to_right(g, left) if g in lower else to_left(g, right)).wait_send()
    outs = [pltpu.make_async_copy(src, dst, out_sem.at[i]) for i, (src, dst) in enumerate(
        ((basis_v, basis_out), (reduced_v, reduced_out)))]
    ritz(col, dense_hi, dense_lo, sums, high_ref, basis_v, reduced_v, inv_v, outs)
    for copy in outs:
        copy.wait()


def hand_out_kernel(basis_in, reduced_in, basis_out, reduced_out, basis_v, reduced_v, in_sem, out_sem):
    parts = [(basis_in.at[pl.ds(8 * i, 8)], basis_v.at[pl.ds(8 * i, 8)], basis_out.at[pl.ds(8 * i, 8)])
             for i in range(COLS // 8)] + [(reduced_in, reduced_v, reduced_out)]
    there = [pltpu.make_async_copy(src, mid, in_sem.at[i]) for i, (src, mid, _) in enumerate(parts)]
    back = [pltpu.make_async_copy(mid, dst, out_sem.at[i]) for i, (_, mid, dst) in enumerate(parts)]
    for copy in there:
        copy.start()
    for first, second in zip(there, back):
        first.wait()
        second.start()
    for copy in back:
        copy.wait()


def local(ntile, block, tiles, intact, adjacency, stiff_diag, cut_low, cut_high):
    zc = min(16, ntile)
    ny = ntile // zc
    share = 2 * COLS // 8
    flat = tiles.reshape(NBLK, 4, 72, LANES).transpose(0, 2, 1, 3).reshape(NBLK * 4 * 72, LANES)
    diag = stiff_diag.reshape(NBLK * TILE // LANES, LANES)
    hbm = pl.BlockSpec(memory_space=pltpu.HBM)
    npair = NBLK // 2
    dma = pltpu.SemaphoreType.DMA
    vec = pltpu.VMEM((COLS, NBLK * LANES), F32)
    halo = pltpu.VMEM((3, COLS, REACH * LANES), F32)
    width = 4 * TILE
    basis, reduced = pl.pallas_call(
        functools.partial(filter_kernel, ntile, zc),
        out_shape=(
            jax.ShapeDtypeStruct((COLS, NBLK * TILE), F32),
            jax.ShapeDtypeStruct((NCOL * COLS, NCOL * COLS), F32),
        ),
        in_specs=[hbm] * 7,
        out_specs=(hbm, hbm),
        scratch_shapes=[
            pltpu.SMEM((4, NBLK), jnp.int32),
            pltpu.SMEM((1,), F32),
            pltpu.SMEM((1,), F32),
            pltpu.VMEM((COLS, NBLK * TILE), F32),
            pltpu.VMEM((NCOL * COLS, NCOL * COLS), F32),
            pltpu.VMEM((NBLK * 4 * 72, LANES), F32),
            pltpu.VMEM((NBLK, 4, TILE), jnp.int32),
            pltpu.VMEM((COLS, NBLK * TILE), F32),
            pltpu.VMEM((NBLK * TILE // LANES, LANES), F32),
            pltpu.VMEM((NBLK * 24, LANES), F32),
            pltpu.VMEM((NBLK * 24, 12 * LANES), F32),
            pltpu.VMEM((LANES, LANES), F32),
            pltpu.VMEM((LANES, LANES), F32),
            pltpu.VMEM((NBLK, LANES), F32),
            pltpu.VMEM((2, REACH, LANES, LANES), F32),
            pltpu.VMEM((npair + 2, 8 * LANES, 2 * LANES), BF16),
            pltpu.VMEM((npair + 2, 8 * LANES, 2 * LANES), BF16),
            vec, vec, vec,
            pltpu.VMEM((2, 2 * COLS, (NBLK + 2 * REACH) * LANES), BF16),
            halo, halo, halo,
            pltpu.VMEM((NCOL, NBLK // 4, COLS, width), F32),
            pltpu.VMEM((NBLK // 4, COLS, width), F32),
            pltpu.VMEM((8, share, LANES), F32),
            pltpu.VMEM((zc, share, LANES), F32),
            pltpu.VMEM((ny, share, LANES), F32),
            pltpu.VMEM((8 * NCOL, share, LANES), F32),
            pltpu.VMEM((NCOL * COLS, NCOL * COLS), F32),
            pltpu.VMEM((NCOL, NBLK // 4, COLS, width), BF16),
            pltpu.VMEM((NCOL, NBLK // 4, COLS, width), BF16),
            dma((4,)), dma((6,)), dma((2,)), dma((3,)), dma((3,)), dma((3,)), dma((3,)),
            dma((18,)), dma((18,)), dma((3,)), dma((3,)),
        ],
        compiler_params=pltpu.CompilerParams(
            collective_id=0, has_side_effects=True, vmem_limit_bytes=57 * 1024 * 1024),
        name="filter",
    )(block, flat, intact, adjacency.T, diag, cut_low, cut_high)
    return pl.pallas_call(
        hand_out_kernel,
        out_shape=(
            jax.ShapeDtypeStruct((COLS, NBLK * TILE), F32),
            jax.ShapeDtypeStruct((NCOL * COLS, NCOL * COLS), F32),
        ),
        in_specs=[hbm, hbm],
        out_specs=(hbm, hbm),
        scratch_shapes=[
            pltpu.VMEM((COLS, NBLK * TILE), F32),
            pltpu.VMEM((NCOL * COLS, NCOL * COLS), F32),
            dma((5,)), dma((5,)),
        ],
        compiler_params=pltpu.CompilerParams(vmem_limit_bytes=57 * 1024 * 1024),
        name="hand_out",
    )(basis, reduced)


def solution(mesh):
    in_specs = (
        P("col", "tile"),
        P("tile", None, None),
        P("tile", None, None),
        P("tile", None),
        P("tile"),
        P(),
        P(),
    )
    out_specs = (P("col", "tile"), P())
    return jax.shard_map(
        functools.partial(local, mesh.shape["tile"]), mesh=mesh, in_specs=in_specs, out_specs=out_specs,
        check_vma=False)
```

```python
import functools

import jax
import jax.numpy as jnp
from jax import lax
from jax.experimental import pallas as pl
from jax.experimental.pallas import tpu as pltpu
from jax.sharding import PartitionSpec as P

HIGH = lax.Precision.HIGHEST
TILE = 96
LANES = 128
NBLK = 24
REACH = 3
COLS = 32
NCOL = 4
MESH = pl.DeviceIdType.MESH
F32 = jnp.float32
BF16 = jnp.bfloat16


def aligned(x, step):
    return x if isinstance(x, int) else pl.multiple_of(x, step)


def roll(x, shift):
    return pltpu.roll(x, shift, 1)


def lane_id(rows):
    return lax.broadcasted_iota(jnp.int32, (rows, LANES), 1)


def spread_lanes(x0, x1, x2):
    lane = lane_id(x0.shape[0])
    b1 = jnp.where(lane < 32, roll(x0, 32), roll(x1, 32))
    b2 = jnp.where(lane < 64, roll(x1, 64), roll(x2, 64))
    return x0, b1, b2, roll(x2, 96)


def pack_lanes(b0, b1, b2, b3):
    lane = lane_id(b0.shape[0])
    x0 = jnp.where(lane < 96, b0, roll(b1, 96))
    x1 = jnp.where(lane < 64, roll(b1, 96), roll(b2, 64))
    x2 = jnp.where(lane < 32, roll(b2, 64), roll(b3, 32))
    return x0, x1, x2


def halves(x):
    hi = x.astype(BF16)
    return hi, (x - hi.astype(F32)).astype(BF16)


def contract(left, right, dims, precision=None):
    return lax.dot_general(left, right, (dims, ((), ())), precision=precision, preferred_element_type=F32)


def inverse_rows(a):
    groups = len(a)
    m = 8 * groups
    a = list(a)
    lane = lax.broadcasted_iota(jnp.int32, (8, m), 1)
    sub = lax.broadcasted_iota(jnp.int32, (8, m), 0)
    pivots = []
    for g in range(groups):
        c = [[jnp.broadcast_to(a[h][:, 8 * g + t:8 * g + t + 1], (8, m)) for h in range(g, groups)] for t in range(8)]
        kept = jnp.ones((8, m), F32)
        for t in range(8):
            k = 8 * g + t
            pivot = jnp.broadcast_to(c[t][0][t:t + 1], (8, m))
            kept = jnp.where(sub == t, pivot, kept)
            inv = 1.0 / pivot
            row = jnp.where(lane == k, 1.0, jnp.broadcast_to(a[g][t:t + 1], (8, m)))
            facts = [x * inv for x in c[t]]
            facts[0] = jnp.where(sub > t, facts[0], 0.0)
            for u in range(t + 1, 8):
                same = jnp.broadcast_to(c[t][0][u:u + 1], (8, m))
                c[u] = [x - f * same for x, f in zip(c[u], facts)]
            for h in range(g, groups):
                old = jnp.where((lane == k) & (sub > t) if h == g else lane == k, 0.0, a[h])
                a[h] = old - facts[h - g] * row
        pivots.append(kept)
    out = []
    for g in range(groups):
        row = sub + 8 * g
        unit = jnp.where(lane < row, a[g], jnp.where(lane == row, 1.0, 0.0))
        out.append(unit / jnp.sqrt(pivots[g]))
    return out


def ritz(col, hi_ref, lo_ref, sums_ref, high_ref, basis_ref, reduced_ref, inv_ref, outs):
    groups = NCOL * COLS // 8
    rows = inverse_rows([sums_ref[8 * (g // 4) + g % 4] for g in range(groups)])
    for g in range(groups):
        inv_ref[8 * g:8 * g + 8, :] = rows[g]
    mine = inv_ref[pl.ds(col * COLS, COLS), :]
    mine = jnp.concatenate(halves(mine), axis=0)
    for g in range(NBLK // 4):
        hi, lo = (jnp.concatenate([ref[c, g] for c in range(NCOL)], axis=0) for ref in (hi_ref, lo_ref))
        width = hi.shape[1]
        both = contract(mine, hi, ((1,), (0,)))
        low = contract(mine[:COLS], lo, ((1,), (0,)))
        basis_ref[:, width * g:width * (g + 1)] = both[:COLS] + (both[COLS:] + low)

    outs[0].start()

    def three(left, right, dims):
        both = contract(jnp.concatenate(left, axis=0), right[0], dims)
        rows = both.shape[0] // 2
        return both[:rows] + (both[rows:] + contract(left[0], right[1], dims))

    inverse = halves(inv_ref[...])
    proj = halves(jnp.concatenate([sums_ref[8 * (g // 4) + 4 + g % 4] for g in range(groups)], axis=0))
    half = halves(three(inverse, proj, ((1,), (0,))))
    reduced_ref[...] = three(half, inverse, ((1,), (1,))) / high_ref[0]
    outs[1].start()


def filter_kernel(
    ntile, zc, block_ref, tiles_ref, intact_ref, adj_hbm, diag_ref, low_hbm, high_hbm,
    basis_out, reduced_out,
    adj_ref, low_ref, high_ref, basis_v, reduced_v, tiles_v, intact_v, block_v, diag_in, marks_k, marks_f, marks_in, marks_v, diag_v, merged, qh, qlo, v0, v1, v2, vh, ahead, spill, spill_out, dense, stiff,
    part, rx1, rx2, sums, inv_v, dense_hi, dense_lo,
    tile_sem, in_sem, out_sem, ahead_send, ahead_recv, spill_send, spill_recv, x_send, x_recv, r_send, r_recv,
):
    tile = lax.axis_index("tile")
    col = lax.axis_index("col")
    ny = ntile // zc
    q = lax.rem(tile, zc)
    y = lax.div(tile, zc)
    following = lax.rem(tile + 1, ntile)
    previous = lax.rem(tile + ntile - 1, ntile)
    right = lax.rem(col + 1, NCOL)
    left = lax.rem(col + 3, NCOL)
    opposite = lax.rem(col + 2, NCOL)
    zpeers = [(y * zc + lax.rem(q + d, zc), col) for d in range(1, zc)]
    ypeers = [(lax.rem(y + d, ny) * zc + q, col) for d in range(1, ny)]
    core = lax.rem(q, 2)

    def near(dz, c, other):
        return (y * zc + lax.rem(q - core + 2 * dz + zc, zc) + (1 - core if other else core), c)

    spread = [near(dz, c, other) for c in (col, right, left, opposite) for dz in (0, 1, -1, -2)
              for other in (False, True)][1:]

    barrier = pltpu.get_barrier_semaphore()
    peers = [(following, col), (previous, col)] + ypeers + zpeers
    peers += [near(dz, c, other) for c in (right, left, opposite) for dz in (-2, -1, 0, 1, 2)
              for other in (False, True)]

    npair = NBLK // 2
    per = 4 * 72
    chunk = 3

    def tile_copy(i):
        rows = pl.ds(i * 2 * chunk * per, 2 * chunk * per)
        return pltpu.make_async_copy(tiles_ref.at[rows], tiles_v.at[rows], tile_sem.at[i])

    order = (3, 0, 1, 2)
    small = [pltpu.make_async_copy(src, dst, in_sem.at[i]) for i, (src, dst) in enumerate(
        ((intact_ref, intact_v), (block_ref, block_v), (diag_ref, diag_in), (adj_hbm, adj_ref), (low_hbm, low_ref),
         (high_hbm, high_ref)))]
    for copy in small:
        copy.start()
    for i in order:
        tile_copy(i).start()
    for peer in peers:
        pl.semaphore_signal(barrier, inc=1, device_id=peer, device_id_type=MESH)

    def window(buf, p, first=0, last=8):
        start = aligned(2 * LANES * p + LANES * first, LANES)
        return vh[buf, :, pl.ds(start, LANES * (last - first))]

    def keep(buf, p, value):
        hi, lo = halves(value)
        lanes = pl.ds(aligned(2 * LANES * p + REACH * LANES, LANES), value.shape[1])
        vh[buf, 0:COLS, lanes] = hi
        vh[buf, COLS:2 * COLS, lanes] = lo

    def pair(p):
        return pl.ds(aligned(2 * LANES * p, 2 * LANES), 2 * LANES)

    merged[...] = jnp.zeros(merged.shape, F32)
    for ref in (qh, qlo):
        for p, w, c in ((0, 0, 0), (0, 1, 0), (0, 2, 0), (0, 1, 1), (0, 2, 1), (1, 0, 0), (npair, 0, 1)):
            ref[p, pl.ds(LANES * w, LANES), pl.ds(LANES * c, LANES)] = jnp.zeros((LANES, LANES), BF16)
    for buf in range(2):
        vh[buf, :, 0:REACH * LANES] = jnp.zeros((2 * COLS, REACH * LANES), BF16)

    nmark = 3 * 4 * LANES
    rows_id = lax.broadcasted_iota(jnp.int32, (16, nmark), 0)
    lanes_id = lax.broadcasted_iota(jnp.int32, (16, nmark), 1)
    slot_at = lax.div(lanes_id, 3 * LANES)
    row_at = lax.div(lax.rem(lanes_id, 3 * LANES), TILE)
    pick = jnp.where(rows_id == 4 * row_at + slot_at, 1.0, 0.0).astype(BF16)
    marks_in[...] = jnp.zeros((LANES, LANES), F32)
    small[0].wait()
    for j in range(NBLK):
        marks_in[4 * j:4 * j + 4, 0:TILE] = intact_v[j].astype(F32)
    marks_v[...] = marks_in[...].T
    lane24 = lane_id(24)

    def gather_marks(j, _):
        total = jnp.zeros((24, LANES), F32)
        for rho in range(4):
            moved = roll(marks_v[pl.ds(rho, 24, stride=4), :], lax.rem(LANES + 4 * rho - 4 * j, LANES))
            total = jnp.where((lane24 >= 4 * rho) & (lane24 < 4 * rho + 4), moved, total)
        marks_k[pl.ds(pl.multiple_of(24 * j, 8), 24), :] = total
        return 0

    lax.fori_loop(0, NBLK, gather_marks, 0, unroll=4)

    def spread_marks(i, _):
        rows = pl.ds(pl.multiple_of(96 * i, 8), 96)
        marks_f[rows, :] = contract(marks_k[rows, 0:16].astype(BF16), pick, ((1,), (0,)))
        return 0

    lax.fori_loop(4, 6, spread_marks, 0, unroll=2)

    small[1].wait()
    valid32 = lane_id(COLS) < TILE
    for g in range(NBLK // 4):
        xs = [block_v[:, pl.ds((3 * g + i) * LANES, LANES)] for i in range(3)]
        for i, piece in enumerate(spread_lanes(*xs)):
            piece = jnp.where(valid32, piece, 0.0)
            v0[:, pl.ds((4 * g + i) * LANES, LANES)] = piece
            hi, lo = halves(piece)
            lanes = pl.ds((4 * g + i + REACH) * LANES, LANES)
            vh[0, 0:COLS, lanes] = hi
            vh[0, COLS:2 * COLS, lanes] = lo
    for copy in small[2:]:
        copy.wait()
    xs = [diag_in[pl.ds(i, NBLK // 4, stride=3), :] for i in range(3)]
    for i, piece in enumerate(spread_lanes(*xs)):
        diag_v[pl.ds(i, NBLK // 4, stride=4), :] = piece

    pl.semaphore_wait(barrier, len(peers))

    def ahead_copy(a, vec):
        return pltpu.make_async_remote_copy(
            src_ref=vec.at[:, pl.ds(0, REACH * LANES)], dst_ref=ahead.at[a], send_sem=ahead_send.at[a],
            recv_sem=ahead_recv.at[a], device_id=(previous, col), device_id_type=MESH)

    ahead_copy(0, v0).start()

    valid24 = lane_id(24) < TILE

    def prepare(p):
        for par in range(2):
            j = 2 * p + par
            rows = pl.ds(24 * j, 24)
            slots = []
            for s in range(4):
                xs = [tiles_v[pl.ds(per * j + 4 * f + s, 24, stride=12), :] for f in range(3)]
                slots.append([x * marks_f[rows, pl.ds((3 * s + f) * LANES, LANES)] for f, x in enumerate(xs)])
            for r in range(REACH):
                here = [jnp.where(adj_ref[s, j] == r + 1, 1.0, 0.0).astype(F32) for s in range(4)]
                xs = []
                for f in range(3):
                    xs.append((slots[0][f] * here[0] + slots[1][f] * here[1])
                              + (slots[2][f] * here[2] + slots[3][f] * here[3]))
                for rho, piece in enumerate(spread_lanes(*xs)):
                    merged[par, r, pl.ds(rho, 24, stride=4), :] = jnp.where(valid24, piece, 0.0)
            for r in range(REACH):
                value = merged[par, r]
                target = par + r + 1
                back_rows = pl.ds(LANES * (par + 3 - 2 * (target // 2)), LANES)
                back_lanes = pl.ds(LANES * (target % 2), LANES)
                hi, lo = halves(value)
                qh[p + target // 2, back_rows, back_lanes] = hi
                qlo[p + target // 2, back_rows, back_lanes] = lo
                front_rows = pl.ds(LANES * (target + 3), LANES)
                hi, lo = halves(value.T)
                qh[p, front_rows, pl.ds(LANES * par, LANES)] = hi
                qlo[p, front_rows, pl.ds(LANES * par, LANES)] = lo
        for ref in (qh, qlo):
            for w, c in ((3, 0), (7, 0), (0, 1), (4, 1)):
                ref[p, pl.ds(LANES * w, LANES), pl.ds(LANES * c, LANES)] = jnp.zeros((LANES, LANES), BF16)

    has_next = tile < ntile - 1
    has_prev = tile > 0
    low = jnp.full((1, 2 * LANES), low_ref[0], F32)
    high = jnp.full((1, 2 * LANES), high_ref[0], F32)
    center = (low + high) / 2.0
    inv_half = 1.0 / ((high - low) / 2.0)

    def product(lhs, hi, lo):
        both = contract(lhs, hi, ((1,), (0,)))
        return both[:COLS] + both[COLS:] + contract(lhs[:COLS], lo, ((1,), (0,)))

    def couple(buf, p, first=0, last=8):
        rows = pl.ds(LANES * first, LANES * (last - first))
        return product(window(buf, p, first, last), qh[p, rows, :], qlo[p, rows, :])

    def spill_copy(a):
        return pltpu.make_async_remote_copy(
            src_ref=spill_out.at[a], dst_ref=spill.at[a], send_sem=spill_send.at[a],
            recv_sem=spill_recv.at[a], device_id=(following, col), device_id_type=MESH)

    def send_spill(a, buf):
        spill_out[a, :, 0:2 * LANES] = couple(buf, npair, 0, 3)
        tail = window(buf, npair, 1, 3)[:, LANES:2 * LANES]
        spill_out[a, :, 2 * LANES:3 * LANES] = product(
            tail, qh[npair + 1, 0:LANES, 0:LANES], qlo[npair + 1, 0:LANES, 0:LANES])
        spill_copy(a).start()

    def stiffness(vec, p, res):
        lanes = pair(p)
        d = jnp.concatenate([diag_v[pl.ds(2 * p, 1), :], diag_v[pl.ds(2 * p + 1, 1), :]], axis=1)
        return d * vec[:, lanes] - res

    def inside(buf, vec, finish, p):
        finish(p, stiffness(vec, p, couple(buf, p)))
        return 0

    def run(buf, vec, finish, first, last):
        lax.fori_loop(first, last, lambda p, _: inside(buf, vec, finish, p), 0, unroll=2)

    def apply(a, buf, vec, finish, runs, hook=None, between=None, after_tails=None):
        for first, last in runs:
            run(buf, vec, finish, first, last)
            if hook is not None:
                hook(first // 2)
        heads = [couple(buf, p) for p in (0, 1)]
        tails = [couple(buf, npair - 2, 0, 6), couple(buf, npair - 1, 0, 4)]
        if between is not None:
            between()
        ahead_copy(a, vec).wait_recv()
        keep(buf, npair, jnp.where(has_next, ahead[a], 0.0))
        tails[0] += couple(buf, npair - 2, 6, 8)
        tails[1] += couple(buf, npair - 1, 4, 8)
        for i in range(2):
            finish(npair - 2 + i, stiffness(vec, npair - 2 + i, tails[i]))
        if after_tails is not None:
            after_tails()
        spill_copy(a).wait_recv()
        extra = jnp.where(has_prev, spill[a], 0.0)
        heads[0] += extra[:, 0:2 * LANES]
        heads[1] += jnp.concatenate([extra[:, 2 * LANES:], jnp.zeros((COLS, LANES), F32)], axis=1)
        for i in range(2):
            finish(i, stiffness(vec, i, heads[i]))
        ahead_copy(a, vec).wait_send()
        spill_copy(a).wait_send()

    def finish_first(p, kv):
        lanes = pair(p)
        value = (kv - center * v0[:, lanes]) * inv_half
        v1[:, lanes] = value
        keep(1, p, value)

    def finish_filtered(p, kv):
        lanes = pair(p)
        value = 2.0 * ((kv - center * v1[:, lanes]) * inv_half) - v0[:, lanes]
        v2[:, lanes] = value
        keep(0, p, value)

    def finish_stiff(p, kv):
        v1[:, pair(p)] = kv

    def compact(src, g):
        return pack_lanes(*[src[:, pl.ds((4 * g + k) * LANES, LANES)] for k in range(4)])

    ngroup = NBLK // 4
    lower = (0, 1, 2)
    upper = (3, 4, 5)

    def x_copy(i, source, g, to):
        return pltpu.make_async_remote_copy(
            src_ref=dense.at[source, g], dst_ref=dense.at[source, g], send_sem=x_send.at[i],
            recv_sem=x_recv.at[i], device_id=(tile, to), device_id_type=MESH)

    def to_right(g, source=None):
        if source is None:
            return x_copy(g, col, g, right)
        return x_copy(2 * ngroup + g, source, g, right)

    def to_left(g, source=None):
        if source is None:
            return x_copy(ngroup + g, col, g, left)
        return x_copy(2 * ngroup + g, source, g, left)

    def pack_group(g):
        for i, x in enumerate(compact(v2, g)):
            dense[col, g, :, LANES * i:LANES * (i + 1)] = x

    def send_group(g):
        pack_group(g)
        to_right(g).start()
        to_left(g).start()

    def pass_on(g):
        if g in lower:
            to_right(g).wait_recv()
            to_right(g, left).start()
        else:
            to_left(g).wait_recv()
            to_left(g, right).start()

    def start_second():
        for g in (2, 3):
            run(1, v1, finish_filtered, 2 * g, 2 * g + 2)
            send_group(g)

    def start_third():
        run(0, v2, finish_stiff, 4, 8)
        pass_on(2)
        pass_on(3)

    def last_relays(g):
        if g == 4:
            pass_on(0)
            pass_on(5)

    for n, i in enumerate(order):
        tile_copy(i).wait()
        for p in range(i * chunk, (i + 1) * chunk):
            prepare(p)
            if 2 < p < npair - chunk:
                inside(0, v0, finish_first, p - 1)
        if n == 0:
            send_spill(0, 0)
            lax.fori_loop(0, 4, spread_marks, 0, unroll=2)
    apply(0, 0, v0, finish_first, ((npair - chunk - 1, npair - 2),), None, start_second,
          lambda: send_spill(1, 1))
    ahead_copy(1, v1).start()
    apply(1, 1, v1, finish_filtered, ((2, 4), (8, 10)), send_group, start_third, lambda: send_spill(2, 0))
    ahead_copy(2, v2).start()
    pack_group(0)
    to_right(0).start()
    pack_group(5)
    to_left(5).start()
    to_right(5).start()
    to_left(0).start()
    pass_on(1)
    pass_on(4)
    apply(2, 0, v2, finish_stiff, ((2, 4), (8, 10)), last_relays)
    for g in range(ngroup):
        for i, x in enumerate(compact(v1, g)):
            stiff[g, :, LANES * i:LANES * (i + 1)] = x

    def split_rows(g):
        hi_f, lo_f = halves(dense[col, g])
        hi_s, lo_s = halves(stiff[g])
        return jnp.concatenate([hi_f, hi_s, lo_f, lo_s], axis=0)

    own = [split_rows(g) for g in range(ngroup)]

    def against(source, groups):
        lhs = jnp.concatenate([own[g] for g in groups], axis=1)
        parts = [halves(dense[source, g]) for g in groups]
        for g, (hi, lo) in zip(groups, parts):
            dense_hi[source, g] = hi
            dense_lo[source, g] = lo
        rhs = jnp.concatenate([jnp.concatenate([x[i] for x in parts], axis=1) for i in range(2)], axis=0)
        res = contract(lhs, rhs, ((1,), (1,)))
        half = 2 * COLS
        return res[:half, :COLS] + res[half:, :COLS] + (res[:half, COLS:] + res[half:, COLS:])

    mine = against(col, lower + upper)
    of_left = against(left, lower)
    of_right = against(right, upper)
    for g in upper:
        to_right(g).wait_recv()
    of_left += against(left, upper)
    for g in lower:
        to_left(g).wait_recv()
    of_right += against(right, lower)
    of_opposite = jnp.zeros((2 * COLS, COLS), F32)
    for groups in ((1, 2, 3, 4), (0, 5)):
        for g in groups:
            (to_right(g, left) if g in lower else to_left(g, right)).wait_recv()
        of_opposite += against(opposite, groups)
    total = jnp.concatenate([mine, of_right, of_opposite, of_left], axis=1)
    total = roll(total, COLS * col) * (1.0 / (NBLK * TILE * ntile))

    nshare = 8
    share = 2 * COLS // nshare
    for i in range(nshare):
        part[i] = total[share * i:share * (i + 1)]

    def r_copy(i, src, dst, to):
        return pltpu.make_async_remote_copy(
            src_ref=src, dst_ref=dst, send_sem=r_send.at[i], recv_sem=r_recv.at[i],
            device_id=to, device_id_type=MESH)

    def arrived(i, ref):
        copy = r_copy(i, ref, ref, (tile, right))
        copy.wait_recv()
        copy.wait_send()

    for d in range(1, zc):
        r_copy(0, part.at[lax.rem(q + d, nshare)], rx1.at[q], zpeers[d - 1]).start()
    own_share = lax.rem(q, nshare)
    rx1[q] = part[own_share]
    arrived(0, rx1.at[pl.ds(0, zc - 1)])
    mine = rx1[0]
    for i in range(1, zc):
        mine += rx1[i]
    rx2[y] = mine
    for peer in ypeers:
        r_copy(1, rx2.at[y], rx2.at[y], peer).start()
    arrived(1, rx2.at[pl.ds(0, ny - 1)])
    mine = rx2[0]
    for i in range(1, ny):
        mine += rx2[i]
    here = nshare * col + own_share
    sums[here] = mine
    for peer in spread:
        r_copy(2, sums.at[here], sums.at[here], peer).start()
    arrived(2, sums.at[pl.ds(0, NCOL * nshare - 1)])
    for g in range(ngroup):
        to_right(g).wait_send()
        to_left(g).wait_send()
        (to_right(g, left) if g in lower else to_left(g, right)).wait_send()
    outs = [pltpu.make_async_copy(src, dst, out_sem.at[i]) for i, (src, dst) in enumerate(
        ((basis_v, basis_out), (reduced_v, reduced_out)))]
    ritz(col, dense_hi, dense_lo, sums, high_ref, basis_v, reduced_v, inv_v, outs)
    for copy in outs:
        copy.wait()


def hand_out_kernel(basis_in, reduced_in, basis_out, reduced_out, basis_v, reduced_v, in_sem, out_sem):
    parts = [(basis_in.at[pl.ds(8 * i, 8)], basis_v.at[pl.ds(8 * i, 8)], basis_out.at[pl.ds(8 * i, 8)])
             for i in range(COLS // 8)] + [(reduced_in, reduced_v, reduced_out)]
    there = [pltpu.make_async_copy(src, mid, in_sem.at[i]) for i, (src, mid, _) in enumerate(parts)]
    back = [pltpu.make_async_copy(mid, dst, out_sem.at[i]) for i, (_, mid, dst) in enumerate(parts)]
    for copy in there:
        copy.start()
    for first, second in zip(there, back):
        first.wait()
        second.start()
    for copy in back:
        copy.wait()


def local(ntile, block, tiles, intact, adjacency, stiff_diag, cut_low, cut_high):
    zc = min(16, ntile)
    ny = ntile // zc
    share = 2 * COLS // 8
    flat = tiles.reshape(NBLK, 4, 72, LANES).transpose(0, 2, 1, 3).reshape(NBLK * 4 * 72, LANES)
    diag = stiff_diag.reshape(NBLK * TILE // LANES, LANES)
    hbm = pl.BlockSpec(memory_space=pltpu.HBM)
    npair = NBLK // 2
    dma = pltpu.SemaphoreType.DMA
    vec = pltpu.VMEM((COLS, NBLK * LANES), F32)
    halo = pltpu.VMEM((3, COLS, REACH * LANES), F32)
    width = 4 * TILE
    basis, reduced = pl.pallas_call(
        functools.partial(filter_kernel, ntile, zc),
        out_shape=(
            jax.ShapeDtypeStruct((COLS, NBLK * TILE), F32),
            jax.ShapeDtypeStruct((NCOL * COLS, NCOL * COLS), F32),
        ),
        in_specs=[hbm] * 7,
        out_specs=(hbm, hbm),
        scratch_shapes=[
            pltpu.SMEM((4, NBLK), jnp.int32),
            pltpu.SMEM((1,), F32),
            pltpu.SMEM((1,), F32),
            pltpu.VMEM((COLS, NBLK * TILE), F32),
            pltpu.VMEM((NCOL * COLS, NCOL * COLS), F32),
            pltpu.VMEM((NBLK * 4 * 72, LANES), F32),
            pltpu.VMEM((NBLK, 4, TILE), jnp.int32),
            pltpu.VMEM((COLS, NBLK * TILE), F32),
            pltpu.VMEM((NBLK * TILE // LANES, LANES), F32),
            pltpu.VMEM((NBLK * 24, LANES), F32),
            pltpu.VMEM((NBLK * 24, 12 * LANES), F32),
            pltpu.VMEM((LANES, LANES), F32),
            pltpu.VMEM((LANES, LANES), F32),
            pltpu.VMEM((NBLK, LANES), F32),
            pltpu.VMEM((2, REACH, LANES, LANES), F32),
            pltpu.VMEM((npair + 2, 8 * LANES, 2 * LANES), BF16),
            pltpu.VMEM((npair + 2, 8 * LANES, 2 * LANES), BF16),
            vec, vec, vec,
            pltpu.VMEM((2, 2 * COLS, (NBLK + 2 * REACH) * LANES), BF16),
            halo, halo, halo,
            pltpu.VMEM((NCOL, NBLK // 4, COLS, width), F32),
            pltpu.VMEM((NBLK // 4, COLS, width), F32),
            pltpu.VMEM((8, share, LANES), F32),
            pltpu.VMEM((zc, share, LANES), F32),
            pltpu.VMEM((ny, share, LANES), F32),
            pltpu.VMEM((8 * NCOL, share, LANES), F32),
            pltpu.VMEM((NCOL * COLS, NCOL * COLS), F32),
            pltpu.VMEM((NCOL, NBLK // 4, COLS, width), BF16),
            pltpu.VMEM((NCOL, NBLK // 4, COLS, width), BF16),
            dma((4,)), dma((6,)), dma((2,)), dma((3,)), dma((3,)), dma((3,)), dma((3,)),
            dma((18,)), dma((18,)), dma((3,)), dma((3,)),
        ],
        compiler_params=pltpu.CompilerParams(
            collective_id=0, has_side_effects=True, vmem_limit_bytes=57 * 1024 * 1024),
        name="filter",
    )(block, flat, intact, adjacency.T, diag, cut_low, cut_high)
    return pl.pallas_call(
        hand_out_kernel,
        out_shape=(
            jax.ShapeDtypeStruct((COLS, NBLK * TILE), F32),
            jax.ShapeDtypeStruct((NCOL * COLS, NCOL * COLS), F32),
        ),
        in_specs=[hbm, hbm],
        out_specs=(hbm, hbm),
        scratch_shapes=[
            pltpu.VMEM((COLS, NBLK * TILE), F32),
            pltpu.VMEM((NCOL * COLS, NCOL * COLS), F32),
            dma((5,)), dma((5,)),
        ],
        compiler_params=pltpu.CompilerParams(vmem_limit_bytes=57 * 1024 * 1024),
        name="hand_out",
    )(basis, reduced)


def solution(mesh):
    in_specs = (
        P("col", "tile"),
        P("tile", None, None),
        P("tile", None, None),
        P("tile", None),
        P("tile"),
        P(),
        P(),
    )
    out_specs = (P("col", "tile"), P())
    return jax.shard_map(
        functools.partial(local, mesh.shape["tile"]), mesh=mesh, in_specs=in_specs, out_specs=out_specs,
        check_vma=False)
```

```python
import functools

import jax
import jax.numpy as jnp
from jax import lax
from jax.experimental import pallas as pl
from jax.experimental.pallas import tpu as pltpu
from jax.sharding import PartitionSpec as P

HIGH = lax.Precision.HIGHEST
TILE = 96
LANES = 128
NBLK = 24
REACH = 3
COLS = 32
NCOL = 4
MESH = pl.DeviceIdType.MESH
F32 = jnp.float32
BF16 = jnp.bfloat16


def aligned(x, step):
    return x if isinstance(x, int) else pl.multiple_of(x, step)


def roll(x, shift):
    return pltpu.roll(x, shift, 1)


def lane_id(rows):
    return lax.broadcasted_iota(jnp.int32, (rows, LANES), 1)


def spread_lanes(x0, x1, x2):
    lane = lane_id(x0.shape[0])
    b1 = jnp.where(lane < 32, roll(x0, 32), roll(x1, 32))
    b2 = jnp.where(lane < 64, roll(x1, 64), roll(x2, 64))
    return x0, b1, b2, roll(x2, 96)


def pack_lanes(b0, b1, b2, b3):
    lane = lane_id(b0.shape[0])
    x0 = jnp.where(lane < 96, b0, roll(b1, 96))
    x1 = jnp.where(lane < 64, roll(b1, 96), roll(b2, 64))
    x2 = jnp.where(lane < 32, roll(b2, 64), roll(b3, 32))
    return x0, x1, x2


def halves(x):
    hi = x.astype(BF16)
    return hi, (x - hi.astype(F32)).astype(BF16)


def contract(left, right, dims, precision=None):
    return lax.dot_general(left, right, (dims, ((), ())), precision=precision, preferred_element_type=F32)


def inverse_rows(a):
    groups = len(a)
    m = 8 * groups
    a = list(a)
    lane = lax.broadcasted_iota(jnp.int32, (8, m), 1)
    sub = lax.broadcasted_iota(jnp.int32, (8, m), 0)
    pivots = []
    for g in range(groups):
        c = [[jnp.broadcast_to(a[h][:, 8 * g + t:8 * g + t + 1], (8, m)) for h in range(g, groups)] for t in range(8)]
        kept = jnp.ones((8, m), F32)
        for t in range(8):
            k = 8 * g + t
            pivot = jnp.broadcast_to(c[t][0][t:t + 1], (8, m))
            kept = jnp.where(sub == t, pivot, kept)
            inv = 1.0 / pivot
            row = jnp.where(lane == k, 1.0, jnp.broadcast_to(a[g][t:t + 1], (8, m)))
            facts = [x * inv for x in c[t]]
            facts[0] = jnp.where(sub > t, facts[0], 0.0)
            for u in range(t + 1, 8):
                same = jnp.broadcast_to(c[t][0][u:u + 1], (8, m))
                c[u] = [x - f * same for x, f in zip(c[u], facts)]
            for h in range(g, groups):
                old = jnp.where((lane == k) & (sub > t) if h == g else lane == k, 0.0, a[h])
                a[h] = old - facts[h - g] * row
        pivots.append(kept)
    out = []
    for g in range(groups):
        row = sub + 8 * g
        unit = jnp.where(lane < row, a[g], jnp.where(lane == row, 1.0, 0.0))
        out.append(unit / jnp.sqrt(pivots[g]))
    return out


def ritz(col, hi_ref, lo_ref, sums_ref, high_ref, basis_ref, reduced_ref, inv_ref, outs):
    groups = NCOL * COLS // 8
    rows = inverse_rows([sums_ref[8 * (g // 4) + g % 4] for g in range(groups)])
    for g in range(groups):
        inv_ref[8 * g:8 * g + 8, :] = rows[g]
    mine = inv_ref[pl.ds(col * COLS, COLS), :]
    mine = jnp.concatenate(halves(mine), axis=0)
    for g in range(NBLK // 4):
        hi, lo = (jnp.concatenate([ref[c, g] for c in range(NCOL)], axis=0) for ref in (hi_ref, lo_ref))
        width = hi.shape[1]
        both = contract(mine, hi, ((1,), (0,)))
        low = contract(mine[:COLS], lo, ((1,), (0,)))
        basis_ref[:, width * g:width * (g + 1)] = both[:COLS] + (both[COLS:] + low)

    outs[0].start()

    def three(left, right, dims):
        both = contract(jnp.concatenate(left, axis=0), right[0], dims)
        rows = both.shape[0] // 2
        return both[:rows] + (both[rows:] + contract(left[0], right[1], dims))

    inverse = halves(inv_ref[...])
    proj = halves(jnp.concatenate([sums_ref[8 * (g // 4) + 4 + g % 4] for g in range(groups)], axis=0))
    half = halves(three(inverse, proj, ((1,), (0,))))
    reduced_ref[...] = three(half, inverse, ((1,), (1,))) / high_ref[0]
    outs[1].start()


def filter_kernel(
    ntile, zc, block_ref, tiles_ref, intact_ref, adj_hbm, diag_ref, low_hbm, high_hbm,
    basis_out, reduced_out,
    adj_ref, low_ref, high_ref, basis_v, reduced_v, tiles_v, intact_v, block_v, diag_in, marks_k, marks_f, marks_in, marks_v, diag_v, merged, qh, qlo, v0, v1, v2, vh, ahead, spill, spill_out, dense, stiff,
    part, rx1, rx2, sums, inv_v, dense_hi, dense_lo,
    tile_sem, in_sem, out_sem, ahead_send, ahead_recv, spill_send, spill_recv, x_send, x_recv, r_send, r_recv,
):
    tile = lax.axis_index("tile")
    col = lax.axis_index("col")
    ny = ntile // zc
    q = lax.rem(tile, zc)
    y = lax.div(tile, zc)
    following = lax.rem(tile + 1, ntile)
    previous = lax.rem(tile + ntile - 1, ntile)
    right = lax.rem(col + 1, NCOL)
    left = lax.rem(col + 3, NCOL)
    opposite = lax.rem(col + 2, NCOL)
    zpeers = [(y * zc + lax.rem(q + d, zc), col) for d in range(1, zc)]
    ypeers = [(lax.rem(y + d, ny) * zc + q, col) for d in range(1, ny)]
    core = lax.rem(q, 2)

    def near(dz, c, other):
        return (y * zc + lax.rem(q - core + 2 * dz + zc, zc) + (1 - core if other else core), c)

    spread = [near(dz, c, other) for c in (col, right, left, opposite) for dz in (0, 1, -1, -2)
              for other in (False, True)][1:]

    barrier = pltpu.get_barrier_semaphore()
    peers = [(following, col), (previous, col)] + ypeers + zpeers
    peers += [near(dz, c, other) for c in (right, left, opposite) for dz in (-2, -1, 0, 1, 2)
              for other in (False, True)]

    npair = NBLK // 2
    per = 4 * 72
    chunk = 3

    def tile_copy(i):
        rows = pl.ds(i * 2 * chunk * per, 2 * chunk * per)
        return pltpu.make_async_copy(tiles_ref.at[rows], tiles_v.at[rows], tile_sem.at[i])

    order = (3, 0, 1, 2)
    small = [pltpu.make_async_copy(src, dst, in_sem.at[i]) for i, (src, dst) in enumerate(
        ((intact_ref, intact_v), (block_ref, block_v), (diag_ref, diag_in), (adj_hbm, adj_ref), (low_hbm, low_ref),
         (high_hbm, high_ref)))]
    for copy in small:
        copy.start()
    for i in order:
        tile_copy(i).start()
    for peer in peers:
        pl.semaphore_signal(barrier, inc=1, device_id=peer, device_id_type=MESH)

    def window(buf, p, first=0, last=8):
        start = aligned(2 * LANES * p + LANES * first, LANES)
        return vh[buf, :, pl.ds(start, LANES * (last - first))]

    def keep(buf, p, value):
        hi, lo = halves(value)
        lanes = pl.ds(aligned(2 * LANES * p + REACH * LANES, LANES), value.shape[1])
        vh[buf, 0:COLS, lanes] = hi
        vh[buf, COLS:2 * COLS, lanes] = lo

    def pair(p):
        return pl.ds(aligned(2 * LANES * p, 2 * LANES), 2 * LANES)

    merged[...] = jnp.zeros(merged.shape, F32)
    for ref in (qh, qlo):
        for p, w, c in ((0, 0, 0), (0, 1, 0), (0, 2, 0), (0, 1, 1), (0, 2, 1), (1, 0, 0), (npair, 0, 1)):
            ref[p, pl.ds(LANES * w, LANES), pl.ds(LANES * c, LANES)] = jnp.zeros((LANES, LANES), BF16)
    for buf in range(2):
        vh[buf, :, 0:REACH * LANES] = jnp.zeros((2 * COLS, REACH * LANES), BF16)

    nmark = 3 * 4 * LANES
    rows_id = lax.broadcasted_iota(jnp.int32, (16, nmark), 0)
    lanes_id = lax.broadcasted_iota(jnp.int32, (16, nmark), 1)
    slot_at = lax.div(lanes_id, 3 * LANES)
    row_at = lax.div(lax.rem(lanes_id, 3 * LANES), TILE)
    pick = jnp.where(rows_id == 4 * row_at + slot_at, 1.0, 0.0).astype(BF16)
    marks_in[...] = jnp.zeros((LANES, LANES), F32)
    small[0].wait()
    for j in range(NBLK):
        marks_in[4 * j:4 * j + 4, 0:TILE] = intact_v[j].astype(F32)
    marks_v[...] = marks_in[...].T
    lane24 = lane_id(24)

    def gather_marks(j, _):
        total = jnp.zeros((24, LANES), F32)
        for rho in range(4):
            moved = roll(marks_v[pl.ds(rho, 24, stride=4), :], lax.rem(LANES + 4 * rho - 4 * j, LANES))
            total = jnp.where((lane24 >= 4 * rho) & (lane24 < 4 * rho + 4), moved, total)
        marks_k[pl.ds(pl.multiple_of(24 * j, 8), 24), :] = total
        return 0

    lax.fori_loop(0, NBLK, gather_marks, 0, unroll=4)

    def spread_marks(i, _):
        rows = pl.ds(pl.multiple_of(96 * i, 8), 96)
        marks_f[rows, :] = contract(marks_k[rows, 0:16].astype(BF16), pick, ((1,), (0,)))
        return 0

    lax.fori_loop(4, 6, spread_marks, 0, unroll=2)

    small[1].wait()
    valid32 = lane_id(COLS) < TILE
    for g in range(NBLK // 4):
        xs = [block_v[:, pl.ds((3 * g + i) * LANES, LANES)] for i in range(3)]
        for i, piece in enumerate(spread_lanes(*xs)):
            piece = jnp.where(valid32, piece, 0.0)
            v0[:, pl.ds((4 * g + i) * LANES, LANES)] = piece
            hi, lo = halves(piece)
            lanes = pl.ds((4 * g + i + REACH) * LANES, LANES)
            vh[0, 0:COLS, lanes] = hi
            vh[0, COLS:2 * COLS, lanes] = lo
    for copy in small[2:]:
        copy.wait()
    xs = [diag_in[pl.ds(i, NBLK // 4, stride=3), :] for i in range(3)]
    for i, piece in enumerate(spread_lanes(*xs)):
        diag_v[pl.ds(i, NBLK // 4, stride=4), :] = piece

    pl.semaphore_wait(barrier, len(peers))

    def ahead_copy(a, vec):
        return pltpu.make_async_remote_copy(
            src_ref=vec.at[:, pl.ds(0, REACH * LANES)], dst_ref=ahead.at[a], send_sem=ahead_send.at[a],
            recv_sem=ahead_recv.at[a], device_id=(previous, col), device_id_type=MESH)

    ahead_copy(0, v0).start()

    valid24 = lane_id(24) < TILE

    def prepare(p):
        for par in range(2):
            j = 2 * p + par
            rows = pl.ds(24 * j, 24)
            slots = []
            for s in range(4):
                xs = [tiles_v[pl.ds(per * j + 4 * f + s, 24, stride=12), :] for f in range(3)]
                slots.append([x * marks_f[rows, pl.ds((3 * s + f) * LANES, LANES)] for f, x in enumerate(xs)])
            for r in range(REACH):
                here = [jnp.where(adj_ref[s, j] == r + 1, 1.0, 0.0).astype(F32) for s in range(4)]
                xs = []
                for f in range(3):
                    xs.append((slots[0][f] * here[0] + slots[1][f] * here[1])
                              + (slots[2][f] * here[2] + slots[3][f] * here[3]))
                for rho, piece in enumerate(spread_lanes(*xs)):
                    merged[par, r, pl.ds(rho, 24, stride=4), :] = jnp.where(valid24, piece, 0.0)
            for r in range(REACH):
                value = merged[par, r]
                target = par + r + 1
                back_rows = pl.ds(LANES * (par + 3 - 2 * (target // 2)), LANES)
                back_lanes = pl.ds(LANES * (target % 2), LANES)
                hi, lo = halves(value)
                qh[p + target // 2, back_rows, back_lanes] = hi
                qlo[p + target // 2, back_rows, back_lanes] = lo
                front_rows = pl.ds(LANES * (target + 3), LANES)
                hi, lo = halves(value.T)
                qh[p, front_rows, pl.ds(LANES * par, LANES)] = hi
                qlo[p, front_rows, pl.ds(LANES * par, LANES)] = lo
        for ref in (qh, qlo):
            for w, c in ((3, 0), (7, 0), (0, 1), (4, 1)):
                ref[p, pl.ds(LANES * w, LANES), pl.ds(LANES * c, LANES)] = jnp.zeros((LANES, LANES), BF16)

    has_next = tile < ntile - 1
    has_prev = tile > 0
    low = jnp.full((1, 2 * LANES), low_ref[0], F32)
    high = jnp.full((1, 2 * LANES), high_ref[0], F32)
    center = (low + high) / 2.0
    inv_half = 1.0 / ((high - low) / 2.0)

    def product(lhs, hi, lo):
        both = contract(lhs, hi, ((1,), (0,)))
        return both[:COLS] + both[COLS:] + contract(lhs[:COLS], lo, ((1,), (0,)))

    def couple(buf, p, first=0, last=8):
        rows = pl.ds(LANES * first, LANES * (last - first))
        return product(window(buf, p, first, last), qh[p, rows, :], qlo[p, rows, :])

    def spill_copy(a):
        return pltpu.make_async_remote_copy(
            src_ref=spill_out.at[a], dst_ref=spill.at[a], send_sem=spill_send.at[a],
            recv_sem=spill_recv.at[a], device_id=(following, col), device_id_type=MESH)

    def send_spill(a, buf):
        spill_out[a, :, 0:2 * LANES] = couple(buf, npair, 0, 3)
        tail = window(buf, npair, 1, 3)[:, LANES:2 * LANES]
        spill_out[a, :, 2 * LANES:3 * LANES] = product(
            tail, qh[npair + 1, 0:LANES, 0:LANES], qlo[npair + 1, 0:LANES, 0:LANES])
        spill_copy(a).start()

    def stiffness(vec, p, res):
        lanes = pair(p)
        d = jnp.concatenate([diag_v[pl.ds(2 * p, 1), :], diag_v[pl.ds(2 * p + 1, 1), :]], axis=1)
        return d * vec[:, lanes] - res

    def inside(buf, vec, finish, p):
        finish(p, stiffness(vec, p, couple(buf, p)))
        return 0

    def run(buf, vec, finish, first, last):
        lax.fori_loop(first, last, lambda p, _: inside(buf, vec, finish, p), 0, unroll=2)

    def apply(a, buf, vec, finish, runs, hook=None, between=None, after_tails=None,
              after_heads=None):
        for first, last in runs:
            run(buf, vec, finish, first, last)
            if hook is not None:
                hook(first // 2)
        heads = [couple(buf, p) for p in (0, 1)]
        tails = [couple(buf, npair - 2, 0, 6), couple(buf, npair - 1, 0, 4)]
        if between is not None:
            between()

        def end_tails():
            ahead_copy(a, vec).wait_recv()
            keep(buf, npair, jnp.where(has_next, ahead[a], 0.0))
            late = [couple(buf, npair - 2, 6, 8), couple(buf, npair - 1, 4, 8)]
            for i in range(2):
                finish(npair - 2 + i, stiffness(vec, npair - 2 + i, tails[i] + late[i]))
            if after_tails is not None:
                after_tails()

        def end_heads():
            spill_copy(a).wait_recv()
            extra = jnp.where(has_prev, spill[a], 0.0)
            finish(0, stiffness(vec, 0, heads[0] + extra[:, 0:2 * LANES]))
            rest = jnp.concatenate([extra[:, 2 * LANES:], jnp.zeros((COLS, LANES), F32)], axis=1)
            finish(1, stiffness(vec, 1, heads[1] + rest))
            if after_heads is not None:
                after_heads()

        if a == 1:
            end_heads()
            end_tails()
        else:
            end_tails()
            end_heads()
        ahead_copy(a, vec).wait_send()
        spill_copy(a).wait_send()

    def finish_first(p, kv):
        lanes = pair(p)
        value = (kv - center * v0[:, lanes]) * inv_half
        v1[:, lanes] = value
        keep(1, p, value)

    def finish_filtered(p, kv):
        lanes = pair(p)
        value = 2.0 * ((kv - center * v1[:, lanes]) * inv_half) - v0[:, lanes]
        v2[:, lanes] = value
        keep(0, p, value)

    def finish_stiff(p, kv):
        v1[:, pair(p)] = kv

    def compact(src, g):
        return pack_lanes(*[src[:, pl.ds((4 * g + k) * LANES, LANES)] for k in range(4)])

    ngroup = NBLK // 4
    lower = (0, 1, 2)
    upper = (3, 4, 5)

    def x_copy(i, source, g, to):
        return pltpu.make_async_remote_copy(
            src_ref=dense.at[source, g], dst_ref=dense.at[source, g], send_sem=x_send.at[i],
            recv_sem=x_recv.at[i], device_id=(tile, to), device_id_type=MESH)

    def to_right(g, source=None):
        if source is None:
            return x_copy(g, col, g, right)
        return x_copy(2 * ngroup + g, source, g, right)

    def to_left(g, source=None):
        if source is None:
            return x_copy(ngroup + g, col, g, left)
        return x_copy(2 * ngroup + g, source, g, left)

    def pack_group(g):
        for i, x in enumerate(compact(v2, g)):
            dense[col, g, :, LANES * i:LANES * (i + 1)] = x

    def send_group(g):
        pack_group(g)
        to_right(g).start()
        to_left(g).start()

    def pass_on(g):
        if g in lower:
            to_right(g).wait_recv()
            to_right(g, left).start()
        else:
            to_left(g).wait_recv()
            to_left(g, right).start()

    def start_second():
        for g in (2, 3):
            run(1, v1, finish_filtered, 2 * g, 2 * g + 2)
            send_group(g)

    def start_third():
        run(0, v2, finish_stiff, 4, 8)
        pass_on(2)
        pass_on(3)

    def last_relays(g):
        if g == 4:
            pass_on(0)
            pass_on(5)

    for n, i in enumerate(order):
        tile_copy(i).wait()
        for p in range(i * chunk, (i + 1) * chunk):
            prepare(p)
            if 2 < p < npair - chunk:
                inside(0, v0, finish_first, p - 1)
        if n == 0:
            send_spill(0, 0)
            lax.fori_loop(0, 4, spread_marks, 0, unroll=2)
    apply(0, 0, v0, finish_first, ((npair - chunk - 1, npair - 2),), None, start_second,
          lambda: send_spill(1, 1), lambda: ahead_copy(1, v1).start())

    def after_second_tails():
        pack_group(5)
        to_left(5).start()
        to_right(5).start()
        send_spill(2, 0)

    def after_second_heads():
        send_group(0)
        ahead_copy(2, v2).start()

    apply(1, 1, v1, finish_filtered, ((2, 4), (8, 10)), send_group, start_third, after_second_tails, after_second_heads)
    pass_on(1)
    pass_on(4)
    apply(2, 0, v2, finish_stiff, ((2, 4), (8, 10)), last_relays)
    for g in range(ngroup):
        for i, x in enumerate(compact(v1, g)):
            stiff[g, :, LANES * i:LANES * (i + 1)] = x

    def split_rows(g):
        hi_f, lo_f = halves(dense[col, g])
        hi_s, lo_s = halves(stiff[g])
        return jnp.concatenate([hi_f, hi_s, lo_f, lo_s], axis=0)

    own = [split_rows(g) for g in range(ngroup)]

    def against(source, groups):
        lhs = jnp.concatenate([own[g] for g in groups], axis=1)
        parts = [halves(dense[source, g]) for g in groups]
        for g, (hi, lo) in zip(groups, parts):
            dense_hi[source, g] = hi
            dense_lo[source, g] = lo
        rhs = jnp.concatenate([jnp.concatenate([x[i] for x in parts], axis=1) for i in range(2)], axis=0)
        res = contract(lhs, rhs, ((1,), (1,)))
        half = 2 * COLS
        return res[:half, :COLS] + res[half:, :COLS] + (res[:half, COLS:] + res[half:, COLS:])

    mine = against(col, lower + upper)
    of_left = against(left, lower)
    of_right = against(right, upper)
    for g in upper:
        to_right(g).wait_recv()
    of_left += against(left, upper)
    for g in lower:
        to_left(g).wait_recv()
    of_right += against(right, lower)
    of_opposite = jnp.zeros((2 * COLS, COLS), F32)
    for groups in ((1, 2, 3, 4), (0, 5)):
        for g in groups:
            (to_right(g, left) if g in lower else to_left(g, right)).wait_recv()
        of_opposite += against(opposite, groups)
    total = jnp.concatenate([mine, of_right, of_opposite, of_left], axis=1)
    total = roll(total, COLS * col) * (1.0 / (NBLK * TILE * ntile))

    nshare = 8
    share = 2 * COLS // nshare
    for i in range(nshare):
        part[i] = total[share * i:share * (i + 1)]

    def r_copy(i, src, dst, to):
        return pltpu.make_async_remote_copy(
            src_ref=src, dst_ref=dst, send_sem=r_send.at[i], recv_sem=r_recv.at[i],
            device_id=to, device_id_type=MESH)

    def arrived(i, ref):
        copy = r_copy(i, ref, ref, (tile, right))
        copy.wait_recv()
        copy.wait_send()

    for d in range(1, zc):
        r_copy(0, part.at[lax.rem(q + d, nshare)], rx1.at[q], zpeers[d - 1]).start()
    own_share = lax.rem(q, nshare)
    rx1[q] = part[own_share]
    arrived(0, rx1.at[pl.ds(0, zc - 1)])
    mine = rx1[0]
    for i in range(1, zc):
        mine += rx1[i]
    rx2[y] = mine
    for peer in ypeers:
        r_copy(1, rx2.at[y], rx2.at[y], peer).start()
    arrived(1, rx2.at[pl.ds(0, ny - 1)])
    mine = rx2[0]
    for i in range(1, ny):
        mine += rx2[i]
    here = nshare * col + own_share
    sums[here] = mine
    for peer in spread:
        r_copy(2, sums.at[here], sums.at[here], peer).start()
    arrived(2, sums.at[pl.ds(0, NCOL * nshare - 1)])
    for g in range(ngroup):
        to_right(g).wait_send()
        to_left(g).wait_send()
        (to_right(g, left) if g in lower else to_left(g, right)).wait_send()
    outs = [pltpu.make_async_copy(src, dst, out_sem.at[i]) for i, (src, dst) in enumerate(
        ((basis_v, basis_out), (reduced_v, reduced_out)))]
    ritz(col, dense_hi, dense_lo, sums, high_ref, basis_v, reduced_v, inv_v, outs)
    for copy in outs:
        copy.wait()


def hand_out_kernel(basis_in, reduced_in, basis_out, reduced_out, basis_v, reduced_v, in_sem, out_sem):
    parts = [(basis_in.at[pl.ds(8 * i, 8)], basis_v.at[pl.ds(8 * i, 8)], basis_out.at[pl.ds(8 * i, 8)])
             for i in range(COLS // 8)] + [(reduced_in, reduced_v, reduced_out)]
    there = [pltpu.make_async_copy(src, mid, in_sem.at[i]) for i, (src, mid, _) in enumerate(parts)]
    back = [pltpu.make_async_copy(mid, dst, out_sem.at[i]) for i, (_, mid, dst) in enumerate(parts)]
    for copy in there:
        copy.start()
    for first, second in zip(there, back):
        first.wait()
        second.start()
    for copy in back:
        copy.wait()


def local(ntile, block, tiles, intact, adjacency, stiff_diag, cut_low, cut_high):
    zc = min(16, ntile)
    ny = ntile // zc
    share = 2 * COLS // 8
    flat = tiles.reshape(NBLK, 4, 72, LANES).transpose(0, 2, 1, 3).reshape(NBLK * 4 * 72, LANES)
    diag = stiff_diag.reshape(NBLK * TILE // LANES, LANES)
    hbm = pl.BlockSpec(memory_space=pltpu.HBM)
    npair = NBLK // 2
    dma = pltpu.SemaphoreType.DMA
    vec = pltpu.VMEM((COLS, NBLK * LANES), F32)
    halo = pltpu.VMEM((3, COLS, REACH * LANES), F32)
    width = 4 * TILE
    basis, reduced = pl.pallas_call(
        functools.partial(filter_kernel, ntile, zc),
        out_shape=(
            jax.ShapeDtypeStruct((COLS, NBLK * TILE), F32),
            jax.ShapeDtypeStruct((NCOL * COLS, NCOL * COLS), F32),
        ),
        in_specs=[hbm] * 7,
        out_specs=(hbm, hbm),
        scratch_shapes=[
            pltpu.SMEM((4, NBLK), jnp.int32),
            pltpu.SMEM((1,), F32),
            pltpu.SMEM((1,), F32),
            pltpu.VMEM((COLS, NBLK * TILE), F32),
            pltpu.VMEM((NCOL * COLS, NCOL * COLS), F32),
            pltpu.VMEM((NBLK * 4 * 72, LANES), F32),
            pltpu.VMEM((NBLK, 4, TILE), jnp.int32),
            pltpu.VMEM((COLS, NBLK * TILE), F32),
            pltpu.VMEM((NBLK * TILE // LANES, LANES), F32),
            pltpu.VMEM((NBLK * 24, LANES), F32),
            pltpu.VMEM((NBLK * 24, 12 * LANES), F32),
            pltpu.VMEM((LANES, LANES), F32),
            pltpu.VMEM((LANES, LANES), F32),
            pltpu.VMEM((NBLK, LANES), F32),
            pltpu.VMEM((2, REACH, LANES, LANES), F32),
            pltpu.VMEM((npair + 2, 8 * LANES, 2 * LANES), BF16),
            pltpu.VMEM((npair + 2, 8 * LANES, 2 * LANES), BF16),
            vec, vec, vec,
            pltpu.VMEM((2, 2 * COLS, (NBLK + 2 * REACH) * LANES), BF16),
            halo, halo, halo,
            pltpu.VMEM((NCOL, NBLK // 4, COLS, width), F32),
            pltpu.VMEM((NBLK // 4, COLS, width), F32),
            pltpu.VMEM((8, share, LANES), F32),
            pltpu.VMEM((zc, share, LANES), F32),
            pltpu.VMEM((ny, share, LANES), F32),
            pltpu.VMEM((8 * NCOL, share, LANES), F32),
            pltpu.VMEM((NCOL * COLS, NCOL * COLS), F32),
            pltpu.VMEM((NCOL, NBLK // 4, COLS, width), BF16),
            pltpu.VMEM((NCOL, NBLK // 4, COLS, width), BF16),
            dma((4,)), dma((6,)), dma((2,)), dma((3,)), dma((3,)), dma((3,)), dma((3,)),
            dma((18,)), dma((18,)), dma((3,)), dma((3,)),
        ],
        compiler_params=pltpu.CompilerParams(
            collective_id=0, has_side_effects=True, vmem_limit_bytes=57 * 1024 * 1024),
        name="filter",
    )(block, flat, intact, adjacency.T, diag, cut_low, cut_high)
    return pl.pallas_call(
        hand_out_kernel,
        out_shape=(
            jax.ShapeDtypeStruct((COLS, NBLK * TILE), F32),
            jax.ShapeDtypeStruct((NCOL * COLS, NCOL * COLS), F32),
        ),
        in_specs=[hbm, hbm],
        out_specs=(hbm, hbm),
        scratch_shapes=[
            pltpu.VMEM((COLS, NBLK * TILE), F32),
            pltpu.VMEM((NCOL * COLS, NCOL * COLS), F32),
            dma((5,)), dma((5,)),
        ],
        compiler_params=pltpu.CompilerParams(vmem_limit_bytes=57 * 1024 * 1024),
        name="hand_out",
    )(basis, reduced)


def solution(mesh):
    in_specs = (
        P("col", "tile"),
        P("tile", None, None),
        P("tile", None, None),
        P("tile", None),
        P("tile"),
        P(),
        P(),
    )
    out_specs = (P("col", "tile"), P())
    return jax.shard_map(
        functools.partial(local, mesh.shape["tile"]), mesh=mesh, in_specs=in_specs, out_specs=out_specs,
        check_vma=False)
```
